128 devices in a mesh: shard: 32 (over z, x, core), grp: 4 (over y).
Axes of the slice: x: 4, y: 4, z: 4, core: 2. Of those that a mesh axis runs over, the one named last changes fastest.
Arguments:
- query_states: bfloat16 [512, 32, 1024], P(('shard', 'grp')), may hold values from -6 to 6
- norm_gain: float32 [1024], replicated, may hold values from 0.25 to 1.75
- final_gain: float32 [1024], replicated, may hold values from 0.25 to 1.75
- w_gate: bfloat16 [1024, 2624], P(None, 'grp'), may hold values from -0.1875 to 0.1875
- w_up: bfloat16 [1024, 2624], P(None, 'grp'), may hold values from -0.1875 to 0.1875
- w_down_t: bfloat16 [1024, 2624], P(None, 'grp'), may hold values from -0.125 to 0.125
- w_proj: bfloat16 [1024, 128], replicated, may hold values from -0.1875 to 0.1875
- centroids: bfloat16 [128, 262144], P('grp'), may hold values from -0.52734375 to 0.52734375
- bucket_values: float32 [4, 128], P(None, 'grp'), may hold values from -0.26516503 to 0.26516503
- centroid_ids: int32 [4096, 128], P('shard'), may hold values from 0 to 262143
- residual_codes: int32 [4096, 16, 128], P('shard', 'grp'), may hold values from 0 to 65535
- passage_lens: int32 [4096], replicated, may hold values from 16 to 128
- negative_ids: int32 [512, 16], P(('shard', 'grp')), may hold values from 0 to 4095, as said below
Outputs:
- losses: float32 [512], P(('shard', 'grp'))
- grad_gate: float32 [1024, 2624], P('shard', 'grp')
- grad_up: float32 [1024, 2624], P('shard', 'grp')
- grad_down: float32 [1024, 2624], P('shard', 'grp')
- grad_proj: float32 [1024, 128], P(('shard', 'grp'))
The draws below stay inside these ranges and needn't reach their ends.
Inputs may be any that keep to these rules, and one draw needn't show every extreme that they name: `negative_ids`: passage id p lies in index shard p // 128. The 16 candidates of the 4 queries of one device name at most 4 passages of any one index shard, counted with repeats; one index shard, the same for all devices, is named exactly 4 times by every device.
All inputs are finite; a program needn't handle non-finite values.
Results may differ from the reference program's by a relative error of at most 0.029.
Values may be sent and summed in bfloat16 or wider, within the bound.
A program may use at most 256 MiB of HBM per device.

```python
import math
import jax
import jax.numpy as jnp
from jax import lax

D = 1024
FF = 2624
DIM = 128
CENTROIDS = 262144
TOKP = 128
QL = 32
CANDS = 16
Q_DEV = 4
P_SH = 128
WORDS = 16
QUERIES = 512
PASSAGES = 4096
CAP = 4


def draw_negative_ids(key, part):
    shards = PASSAGES // P_SH
    devs = QUERIES // Q_DEV
    wanted = Q_DEV * CANDS
    total = shards * CAP
    hot_key, perm_key, mix_key, pick_key = jax.random.split(key, 4)
    hot = jax.random.randint(hot_key, (), 0, shards)
    slot_owner = jnp.arange(total, dtype=jnp.int32) // CAP
    perms = jax.vmap(lambda k: jax.random.permutation(k, total))(jax.random.split(perm_key, devs)).astype(jnp.int32)
    scores = perms - jnp.where(slot_owner == hot, total, 0).astype(jnp.int32)[None, :]
    order = jnp.argsort(scores, axis=1, stable=True)[:, :wanted].astype(jnp.int32)
    owners = order // CAP
    mixes = jax.vmap(lambda k: jax.random.permutation(k, wanted))(jax.random.split(mix_key, devs)).astype(jnp.int32)
    owners = jnp.take_along_axis(owners, mixes, axis=1)
    within = jax.random.randint(pick_key, (devs, wanted), 0, P_SH).astype(jnp.int32)
    return (owners * P_SH + within).reshape(QUERIES, CANDS).astype(jnp.int32)


def place_ends(array, rng, least, high):
    index_at = [jax.random.randint(jax.random.fold_in(rng, axis), (), 0, length) for axis, length in enumerate(array.shape)]
    main_axis = array.shape.index(max(array.shape))
    next_to = index_at[:main_axis] + [(index_at[main_axis] + 1) % array.shape[main_axis]] + index_at[main_axis + 1:]
    return array.at[tuple(index_at)].set(least).at[tuple(next_to)].set(high)


def block_levels(stream_key, extent, pieces, smallest, top_value):
    loudness, own = 1.0, jax.random.fold_in(stream_key, 6)
    for position, shards_of in pieces:
        steps = jnp.exp(jax.random.uniform(jax.random.fold_in(own, position), (shards_of,), jnp.float32, smallest / len(pieces), top_value / len(pieces)))
        loudness = loudness * jnp.repeat(steps, extent[position] // shards_of).reshape([-1 if axis == position else 1 for axis in range(len(extent))])
    return loudness


def scatter_about(own_key, extent, deviation, most, cuts=(), kind=jnp.bfloat16):
    factor_of = block_levels(own_key, extent, cuts, -0.22, 0.18) if cuts else 1.0
    entries = jax.random.normal(own_key, extent, jnp.float32) * deviation * factor_of
    return jnp.minimum(jnp.maximum(entries, -most), most).astype(kind)


def setup_inputs(seed: int = 0) -> dict:
    key_of = jax.random.split(jax.random.key(seed), 14)
    query_states = scatter_about(key_of[0], (QUERIES, QL, D), 1.0, 6.0, ((0, 128),))
    norm_gain = jnp.clip(1.0 + 0.15 * jax.random.normal(key_of[1], (D,), jnp.float32), 0.25, 1.75)
    final_gain = jnp.clip(1.0 + 0.15 * jax.random.normal(key_of[2], (D,), jnp.float32), 0.25, 1.75)
    w_gate = scatter_about(key_of[3], (D, FF), D ** -0.5, 0.1875, ((1, 4),))
    w_up = scatter_about(key_of[4], (D, FF), D ** -0.5, 0.1875, ((1, 4),))
    w_down_t = scatter_about(key_of[5], (D, FF), FF ** -0.5, 0.125, ((1, 4),))
    w_proj = scatter_about(key_of[6], (D, DIM), D ** -0.5, 0.1875)
    centroids = scatter_about(key_of[7], (DIM, CENTROIDS), (DIM ** -0.5), 0.52734375, ((0, 4),))
    bucket_values = scatter_about(key_of[8], (4, DIM), (0.5 * DIM ** -0.5), 0.26516503, ((1, 4),), jnp.float32)
    centroid_ids = place_ends(jax.random.randint(key_of[9], (PASSAGES, TOKP), 0, CENTROIDS), jax.random.fold_in(key_of[9], 1), 0, CENTROIDS - 1).astype(jnp.int32)
    residual_codes = place_ends(jax.random.randint(key_of[10], (PASSAGES, WORDS, TOKP), 0, 65536), jax.random.fold_in(key_of[10], 1), 0, 65535).astype(jnp.int32)
    passage_lens = place_ends(jax.random.randint(key_of[11], (PASSAGES,), max(1, TOKP // 8), TOKP + 1), jax.random.fold_in(key_of[11], 1), max(1, TOKP // 8), TOKP).astype(jnp.int32)
    negative_ids = draw_negative_ids(jax.random.fold_in(key_of[13], 71), 0)
    return {"query_states": query_states, "norm_gain": norm_gain, "final_gain": final_gain, "w_gate": w_gate, "w_up": w_up, "w_down_t": w_down_t, "w_proj": w_proj, "centroids": centroids, "bucket_values": bucket_values, "centroid_ids": centroid_ids, "residual_codes": residual_codes, "passage_lens": passage_lens, "negative_ids": negative_ids}


def layer_norm(rows, gain):
    centre = rows - lax.optimization_barrier(jnp.mean(rows, axis=-1, keepdims=True))
    spread = lax.optimization_barrier(jnp.mean(centre * centre, axis=-1, keepdims=True))
    return centre * lax.rsqrt(spread + 1e-05) * gain

def gelu_exact(values):
    return 0.5 * values * (1.0 + jax.scipy.special.erf(values / math.sqrt(2.0)))

def gelu_slope(values):
    cdf = 0.5 * (1.0 + jax.scipy.special.erf(values / math.sqrt(2.0)))
    return cdf + values * jnp.exp(-0.5 * values * values) / math.sqrt(2.0 * math.pi)

def rebuild(pass_ids, table, codes, bucket, cent_ids):
    cids = cent_ids[pass_ids]
    words = codes[pass_ids]
    base = jnp.transpose(jnp.take(table, cids, axis=1), (1, 0, 2)).astype(jnp.float32)
    shifts = (2 * jnp.arange(8)).astype(jnp.int32)
    fields = jnp.bitwise_and(jnp.right_shift(words[:, :, None, :], shifts[None, None, :, None]), 3)
    fields = fields.reshape(words.shape[0], words.shape[1] * 8, words.shape[2])
    resid = jnp.zeros(fields.shape, jnp.float32)
    for level in range(4):
        resid = resid + jnp.where(fields == level, bucket[level][None, :, None], jnp.float32(0.0))
    return (base + resid).astype(jnp.bfloat16)

def unit_docs(raw):
    values = raw.astype(jnp.float32)
    width = values.shape[-2]
    scale = lax.rsqrt(lax.optimization_barrier(jnp.mean(values * values, axis=-2, keepdims=True)) + 1e-06) / math.sqrt(width)
    return (values * scale).astype(jnp.bfloat16)

def candidate_losses(proj_rows, docs, doc_lens):
    width = proj_rows.shape[-1]
    scale = lax.rsqrt(lax.optimization_barrier(jnp.mean(proj_rows * proj_rows, axis=-1, keepdims=True)) + 1e-06) / math.sqrt(width)
    queries = (proj_rows * scale).astype(jnp.bfloat16)
    sims = jnp.einsum('kid,kcdj->kicj', queries.astype(jnp.float32), docs.astype(jnp.float32))
    spots = lax.broadcasted_iota(jnp.int32, (1, 1, 1, docs.shape[-1]), 3)
    valid = spots < doc_lens[:, None, :, None]
    logits = jnp.where(valid, 64.0 * sims, jnp.float32(-1e+30))
    top = lax.stop_gradient(lax.optimization_barrier(jnp.max(logits, axis=-1, keepdims=True)))
    soft = (top[..., 0] + jnp.log(lax.optimization_barrier(jnp.sum(jnp.exp(logits - top), axis=-1)))) / 64.0
    scores = 10.0 * lax.optimization_barrier(jnp.sum(soft, axis=1))
    ctop = lax.stop_gradient(lax.optimization_barrier(jnp.max(scores, axis=-1, keepdims=True)))
    total = ctop[:, 0] + jnp.log(lax.optimization_barrier(jnp.sum(jnp.exp(scores - ctop), axis=-1)))
    return total - scores[:, 0]

def reference(query_states, norm_gain, final_gain, w_gate, w_up, w_down_t, w_proj, centroids, bucket_values, centroid_ids, residual_codes, passage_lens, negative_ids):
    rows = query_states.reshape(-1, D).astype(jnp.float32)
    normed = layer_norm(rows, norm_gain).astype(jnp.bfloat16)
    gate = jnp.dot(normed, w_gate, preferred_element_type=jnp.float32)
    up = jnp.dot(normed, w_up, preferred_element_type=jnp.float32)
    hidden = (gelu_exact(gate) * up).astype(jnp.bfloat16)
    out = rows + lax.dot_general(hidden, w_down_t, (((1,), (1,)), ((), ())), preferred_element_type=jnp.float32)
    final = layer_norm(out, final_gain).astype(jnp.bfloat16)
    proj = jnp.dot(final, w_proj, preferred_element_type=jnp.float32)
    blocks = QUERIES // Q_DEV
    proj_blocks = proj.reshape(blocks, Q_DEV, QL, DIM)
    id_blocks = negative_ids.reshape(blocks, Q_DEV, CANDS)

    def one_block(item):
        proj_part, ids = item
        raw = rebuild(ids.reshape(-1), centroids, residual_codes, bucket_values, centroid_ids)
        docs = unit_docs(raw).reshape(Q_DEV, CANDS, DIM, TOKP)
        lens = passage_lens[ids]
        part_losses, pull = jax.vjp(lambda v: candidate_losses(v, docs, lens), proj_part)
        dpart, = pull(jnp.ones_like(part_losses))
        return (part_losses, dpart)
    losses, dproj = lax.map(one_block, (proj_blocks, id_blocks))
    dproj_b = dproj.reshape(-1, DIM).astype(jnp.bfloat16)
    grad_proj = lax.dot_general(final, dproj_b, (((0,), (0,)), ((), ())), preferred_element_type=jnp.float32)
    dfinal = lax.dot_general(dproj_b, w_proj, (((1,), (1,)), ((), ())), preferred_element_type=jnp.float32)
    _, pull_norm = jax.vjp(lambda v: layer_norm(v, final_gain), out)
    dout, = pull_norm(dfinal)
    dout_b = dout.astype(jnp.bfloat16)
    dhid = jnp.dot(dout_b, w_down_t, preferred_element_type=jnp.float32)
    dgate = (dhid * up * gelu_slope(gate)).astype(jnp.bfloat16)
    dup = (dhid * gelu_exact(gate)).astype(jnp.bfloat16)
    contract = (((0,), (0,)), ((), ()))
    grad_gate = lax.dot_general(normed, dgate, contract, preferred_element_type=jnp.float32)
    grad_up = lax.dot_general(normed, dup, contract, preferred_element_type=jnp.float32)
    grad_down = lax.dot_general(dout_b, hidden, contract, preferred_element_type=jnp.float32)
    return (losses.reshape(QUERIES), grad_gate, grad_up, grad_down, grad_proj)
```

```python
import functools
import math

import jax
import jax.numpy as jnp
from jax import lax
from jax.experimental import pallas as pl
from jax.experimental.pallas import tpu as pltpu
from jax.sharding import PartitionSpec as P

MESH = pl.DeviceIdType.MESH


def layer_norm(rows, gain):
    centre = rows - jnp.mean(rows, axis=-1, keepdims=True)
    spread = jnp.mean(centre * centre, axis=-1, keepdims=True)
    return centre * lax.rsqrt(spread + 1e-05) * gain


def gelu_exact(values):
    return 0.5 * values * (1.0 + jax.scipy.special.erf(values / math.sqrt(2.0)))


def gelu_slope(values):
    cdf = 0.5 * (1.0 + jax.scipy.special.erf(values / math.sqrt(2.0)))
    return cdf + values * jnp.exp(-0.5 * values * values) / math.sqrt(2.0 * math.pi)


def rebuild_kernel(blk_ref, lane_ref, codes_ref, bucket_ref, tab_hbm, out_ref, tab, sem):
    parts = sem.shape[0]
    span = tab.shape[1] // parts
    copies = [
        pltpu.make_async_copy(
            tab_hbm.at[:, pl.ds(i * span, span)], tab.at[:, pl.ds(i * span, span)], sem.at[i]
        )
        for i in range(parts)
    ]
    for copy in copies:
        copy.start()
    for copy in copies:
        copy.wait()
    passages, dims, toks = out_ref.shape
    lane = lax.broadcasted_iota(jnp.int32, (dims, toks), 1)
    shift = 2 * lax.broadcasted_iota(jnp.int32, (8, toks), 0)

    def passage(p, carry):
        spot = jnp.broadcast_to(lane_ref[pl.ds(p, 1), :], (dims, toks))
        base = jnp.zeros((dims, toks), jnp.float32)
        for j in range(toks):
            start = pl.multiple_of(blk_ref[p, j] * 128, 128)
            block = tab[:, pl.ds(start, 128)].astype(jnp.float32)
            base = jnp.where(lane == j, jnp.take_along_axis(block, spot, axis=1), base)
        words = codes_ref[p]
        fields = jnp.concatenate(
            [
                jnp.bitwise_and(
                    jnp.right_shift(jnp.broadcast_to(words[w : w + 1], (8, toks)), shift), 3
                )
                for w in range(dims // 8)
            ],
            axis=0,
        )
        resid = jnp.where(
            fields < 2,
            jnp.where(fields == 0, bucket_ref[0], bucket_ref[1]),
            jnp.where(fields == 2, bucket_ref[2], bucket_ref[3]),
        )
        out_ref[p] = (base + resid).astype(jnp.bfloat16)
        return carry

    lax.fori_loop(0, passages, passage, 0)


def rebuild(cent_ids, codes, bucket, table):
    passages, toks = cent_ids.shape
    dims, count = table.shape
    spread = jnp.broadcast_to(bucket[:, :, None], (4, dims, toks))
    return pl.pallas_call(
        rebuild_kernel,
        out_shape=jax.ShapeDtypeStruct((passages, dims, toks), jnp.bfloat16),
        in_specs=[
            pl.BlockSpec(memory_space=pltpu.SMEM),
            pl.BlockSpec(memory_space=pltpu.VMEM),
            pl.BlockSpec(memory_space=pltpu.VMEM),
            pl.BlockSpec(memory_space=pltpu.VMEM),
            pl.BlockSpec(memory_space=pl.ANY),
        ],
        out_specs=pl.BlockSpec(memory_space=pltpu.VMEM),
        scratch_shapes=[pltpu.VMEM((dims, count), jnp.bfloat16), pltpu.SemaphoreType.DMA((8,))],
        compiler_params=pltpu.CompilerParams(vmem_limit_bytes=36 << 20),
        cost_estimate=pl.CostEstimate(flops=0, bytes_accessed=150_000_000, transcendentals=0),
    )(cent_ids >> 7, cent_ids & 127, codes, spread, table)


def pair_kernel(pass_ref, query_ref, lens_ref, docs_ref, q_ref, pull_ref, score_ref):
    sources, caps, q_len, dim = pull_ref.shape
    toks = docs_ref.shape[3]
    spots = lax.broadcasted_iota(jnp.int32, (q_len, toks), 1)

    def source(d, carry):
        for k in range(caps):
            p = pass_ref[d, k]
            raw = jnp.concatenate([docs_ref[g, p] for g in range(docs_ref.shape[0])], axis=0)
            values = raw.astype(jnp.float32)
            scale = lax.rsqrt(jnp.mean(values * values, axis=0, keepdims=True) + 1e-06) / math.sqrt(dim)
            sims = jnp.dot(q_ref[d, query_ref[d, k]], raw, preferred_element_type=jnp.float32)
            raised = jnp.where(spots < lens_ref[p], jnp.exp(64.0 * (sims * scale)), 0.0)
            total = jnp.sum(raised, axis=1, keepdims=True)
            soft = jnp.sum(jnp.log(total), axis=0, keepdims=True) / 64.0
            weights = (raised * (scale / total)).astype(jnp.bfloat16)
            pull_ref[d, k] = lax.dot_general(
                weights, raw, (((1,), (1,)), ((), ())), preferred_element_type=jnp.float32
            ).astype(jnp.bfloat16)
            score_ref[d, pl.ds(k, 1), :] = jnp.broadcast_to(soft, (1, dim))
        return carry

    lax.fori_loop(0, sources, source, 0)


def pairs(slot_pass, slot_query, lens, docs, queries):
    sources, caps = slot_pass.shape
    q_len, dim = queries.shape[2:]
    return pl.pallas_call(
        pair_kernel,
        out_shape=(
            jax.ShapeDtypeStruct((sources, caps, q_len, dim), jnp.bfloat16),
            jax.ShapeDtypeStruct((sources, caps, dim), jnp.float32),
        ),
        in_specs=[pl.BlockSpec(memory_space=pltpu.SMEM)] * 3
        + [pl.BlockSpec(memory_space=pltpu.VMEM)] * 2,
        out_specs=(pl.BlockSpec(memory_space=pltpu.VMEM),) * 2,
        compiler_params=pltpu.CompilerParams(vmem_limit_bytes=24 << 20),
        cost_estimate=pl.CostEstimate(flops=0, bytes_accessed=40_000_000, transcendentals=0),
    )(slot_pass, slot_query, lens, docs, queries)


def coords(shape):
    me = lax.axis_index("shard")
    return me // (2 * shape), (me // 2) % shape, me % 2, lax.axis_index("grp")


def scatter_kernel(
    side, groups, gate_ref, up_ref, down_ref, proj_ref, gate_out, up_out, down_out, proj_out,
    twin, twin_proj, held, held_proj, land, land_proj, rows_sum, land_grp,
    twin_send, twin_recv, chip_send, chip_recv, grp_send, grp_recv,
):
    z, x, core, grp = coords(side)
    chips = side * side
    chip = z * side + x
    sibling = (chip * 2 + 1 - core, grp)

    def peer(step):
        other = ((z + step // side) % side) * side + (x + step % side) % side
        return other, (other * 2 + core, grp)

    barrier = pltpu.get_barrier_semaphore()
    pl.semaphore_signal(barrier, inc=1, device_id=sibling, device_id_type=MESH)
    for step in range(1, chips):
        pl.semaphore_signal(barrier, inc=1, device_id=peer(step)[1], device_id_type=MESH)
    for step in range(1, groups):
        pl.semaphore_signal(
            barrier, inc=1, device_id=(chip * 2 + core, (grp + step) % groups), device_id_type=MESH
        )
    pl.semaphore_wait(barrier, chips + groups - 1)

    terms = (gate_ref, up_ref, down_ref)

    def swap(src, dst, i):
        return pltpu.make_async_remote_copy(
            src_ref=src, dst_ref=dst, send_sem=twin_send.at[i], recv_sem=twin_recv.at[i],
            device_id=sibling, device_id_type=MESH,
        )

    first = [swap(proj_ref.at[:, 1 - core], twin_proj, 3)]
    first += [swap(terms[i].at[:, 1 - core], twin.at[:, i], i) for i in range(3)]
    for copy in first:
        copy.start()
    first[0].wait_recv()

    def add_proj(c, carry):
        held_proj[c] = proj_ref[c, core] + twin_proj[c]
        return carry

    lax.fori_loop(0, chips, add_proj, 0)
    for i in range(3):
        first[1 + i].wait_recv()

        def add(c, carry):
            held[c, i] = (
                terms[i][c, core].astype(jnp.float32) + twin[c, i].astype(jnp.float32)
            ).astype(jnp.bfloat16)
            return carry

        lax.fori_loop(0, chips, add, 0)

    def send(step, src, dst, kind):
        other, device = peer(step)
        return pltpu.make_async_remote_copy(
            src_ref=src.at[other], dst_ref=dst.at[step - 1],
            send_sem=chip_send.at[kind, step - 1], recv_sem=chip_recv.at[kind, step - 1],
            device_id=device, device_id_type=MESH,
        )

    small = [send(step, held_proj, land_proj, 0) for step in range(1, chips)]
    large = [send(step, held, land, 1) for step in range(1, chips)]
    for copy in small:
        copy.start()
    for copy in large:
        copy.start()
    for copy in small:
        copy.wait_recv()
    total = held_proj[chip]
    for step in range(1, chips):
        total = total + land_proj[step - 1]
    rows_sum[...] = total.reshape(rows_sum.shape)
    last = []
    for step in range(1, groups):
        other = (grp + step) % groups
        last.append(
            pltpu.make_async_remote_copy(
                src_ref=rows_sum.at[other], dst_ref=land_grp.at[step - 1],
                send_sem=grp_send.at[step - 1], recv_sem=grp_recv.at[step - 1],
                device_id=(chip * 2 + core, other), device_id_type=MESH,
            )
        )
        last[-1].start()
    for copy in last:
        copy.wait_recv()
    mine = rows_sum[grp]
    for step in range(1, groups):
        mine = mine + land_grp[step - 1]
    proj_out[...] = mine
    for copy in large:
        copy.wait_recv()
    for i, out in enumerate((gate_out, up_out, down_out)):
        total = held[chip, i].astype(jnp.float32)
        for step in range(1, chips):
            total = total + land[step - 1, i].astype(jnp.float32)
        out[...] = total
    for copy in first + small + large + last:
        copy.wait_send()


def scatter_sums(term_gate, term_up, term_down, proj_term, side):
    groups = lax.axis_size("grp")
    width, part = term_gate.shape
    dim = proj_term.shape[1]
    chips = side * side
    rows = width // (2 * chips)
    terms = [t.reshape(chips, 2, rows, part) for t in (term_gate, term_up, term_down)]
    wide = (chips, 3, rows, part)
    return pl.pallas_call(
        functools.partial(scatter_kernel, side, groups),
        out_shape=(jax.ShapeDtypeStruct((rows, part), jnp.float32),) * 3
        + (jax.ShapeDtypeStruct((rows // groups, dim), jnp.float32),),
        in_specs=[pl.BlockSpec(memory_space=pltpu.VMEM)] * 4,
        out_specs=(pl.BlockSpec(memory_space=pltpu.VMEM),) * 4,
        scratch_shapes=[
            pltpu.VMEM(wide, jnp.bfloat16),
            pltpu.VMEM((chips, rows, dim), jnp.float32),
            pltpu.VMEM(wide, jnp.bfloat16),
            pltpu.VMEM((chips, rows, dim), jnp.float32),
            pltpu.VMEM((chips - 1, 3, rows, part), jnp.bfloat16),
            pltpu.VMEM((chips - 1, rows, dim), jnp.float32),
            pltpu.VMEM((groups, rows // groups, dim), jnp.float32),
            pltpu.VMEM((groups - 1, rows // groups, dim), jnp.float32),
            pltpu.SemaphoreType.DMA((4,)),
            pltpu.SemaphoreType.DMA((4,)),
            pltpu.SemaphoreType.DMA((2, chips - 1)),
            pltpu.SemaphoreType.DMA((2, chips - 1)),
            pltpu.SemaphoreType.DMA((groups - 1,)),
            pltpu.SemaphoreType.DMA((groups - 1,)),
        ],
        compiler_params=pltpu.CompilerParams(
            collective_id=0, has_side_effects=True, vmem_limit_bytes=32 << 20
        ),
        cost_estimate=pl.CostEstimate(flops=0, bytes_accessed=60_000_000, transcendentals=0),
    )(*terms, proj_term.reshape(chips, 2, rows, dim))


def ranks(hits):
    count = hits.shape[1]
    before = lax.broadcasted_iota(jnp.int32, (count, count), 0) < lax.broadcasted_iota(
        jnp.int32, (count, count), 1
    )
    return jnp.dot(
        hits.astype(jnp.bfloat16), before.astype(jnp.bfloat16), preferred_element_type=jnp.float32
    ).astype(jnp.int32)


def slots(hits, caps):
    nth = lax.broadcasted_iota(jnp.int32, (1, caps, 1), 1)
    return hits[:, None, :] & (ranks(hits)[:, None, :] == nth)


def local(
    query_states,
    norm_gain,
    final_gain,
    w_gate,
    w_up,
    w_down_t,
    w_proj,
    centroids,
    bucket_values,
    centroid_ids,
    residual_codes,
    passage_lens,
    negative_ids,
):
    q_dev, q_len, width = query_states.shape
    dim = w_proj.shape[1]
    shards = lax.axis_size("shard")
    groups = lax.axis_size("grp")
    side = math.isqrt(shards // 2)
    cands = negative_ids.shape[1]
    tok_rows = q_dev * q_len
    local_pass = centroid_ids.shape[0]
    caps = 2 * q_dev * cands // shards
    me = lax.axis_index("shard")

    flat_ids = negative_ids.reshape(1, -1)
    column_ids = lax.all_gather(flat_ids, "shard", axis=0, tiled=True)
    rows = query_states.reshape(tok_rows, width).astype(jnp.float32)
    normed = layer_norm(rows, norm_gain).astype(jnp.bfloat16)
    group_rows = lax.all_gather(normed, "grp", axis=0, tiled=True)

    raw = rebuild(centroid_ids, residual_codes, bucket_values, centroids)
    docs = lax.all_gather(raw, "grp", axis=0)

    gate = jnp.dot(group_rows, w_gate, preferred_element_type=jnp.float32)
    up = jnp.dot(group_rows, w_up, preferred_element_type=jnp.float32)
    hidden = (gelu_exact(gate) * up).astype(jnp.bfloat16)
    out = rows + lax.psum_scatter(
        lax.dot_general(
            hidden, w_down_t, (((1,), (1,)), ((), ())), preferred_element_type=jnp.float32
        ),
        "grp",
        scatter_dimension=0,
        tiled=True,
    )
    final = layer_norm(out, final_gain).astype(jnp.bfloat16)
    proj = jnp.dot(final, w_proj, preferred_element_type=jnp.float32)
    length = lax.rsqrt(jnp.mean(proj * proj, axis=-1, keepdims=True) + 1e-06)
    scale = length / math.sqrt(dim)
    queries = (proj * scale).astype(jnp.bfloat16).reshape(1, q_dev, q_len, dim)
    column_queries = lax.all_gather(queries, "shard", axis=0, tiled=True)

    asked = slots(column_ids // local_pass == me, caps)
    places = lax.broadcasted_iota(jnp.int32, (1, 1, q_dev * cands), 2)
    slot_pass = jnp.sum(jnp.where(asked, (column_ids % local_pass)[:, None, :], 0), axis=2)
    slot_query = jnp.sum(jnp.where(asked, places // cands, 0), axis=2)
    lens = lax.dynamic_slice(passage_lens, (me * local_pass,), (local_pass,))
    pull, score = pairs(slot_pass, slot_query, lens, docs, column_queries)
    pull = lax.all_to_all(pull, "shard", split_axis=0, concat_axis=0, tiled=True)
    score = lax.all_to_all(score[:, :, :1], "shard", split_axis=0, concat_axis=0, tiled=True)

    owner = lax.broadcasted_iota(jnp.int32, (shards, 1), 0)
    sent = slots(flat_ids // local_pass == owner, caps)
    filled = jnp.any(sent, axis=2).reshape(1, -1)
    place = jnp.sum(jnp.where(sent, places, 0), axis=2).reshape(1, -1)
    query = lax.broadcasted_iota(jnp.int32, (q_dev, 1), 0)
    mine = filled & (place // cands == query)
    first = mine & (place % cands == 0)
    scores = 10.0 * score.reshape(1, -1)
    top = jnp.max(jnp.where(mine, scores, -jnp.inf), axis=1, keepdims=True)
    raised = jnp.where(mine, jnp.exp(scores - top), 0.0)
    total = jnp.sum(raised, axis=1, keepdims=True)
    losses = (
        top + jnp.log(total) - jnp.sum(jnp.where(first, scores, 0.0), axis=1, keepdims=True)
    ).reshape(q_dev)
    weights = 10.0 * (raised / total - first.astype(jnp.float32))
    high = weights.astype(jnp.bfloat16)
    low = (weights - high.astype(jnp.float32)).astype(jnp.bfloat16)
    both = jnp.dot(
        jnp.concatenate([high, low], axis=0),
        pull.reshape(shards * caps, q_len * dim),
        preferred_element_type=jnp.float32,
    )
    dqueries = (both[:q_dev] + both[q_dev:]).reshape(tok_rows, dim)
    dqueries = dqueries.astype(jnp.bfloat16).astype(jnp.float32)
    along = jnp.mean(dqueries * proj, axis=-1, keepdims=True)
    dproj_b = (scale * (dqueries - proj * (length * length * along))).astype(jnp.bfloat16)

    contract = (((0,), (0,)), ((), ()))
    proj_term = lax.dot_general(final, dproj_b, contract, preferred_element_type=jnp.float32)
    dfinal = lax.dot_general(
        dproj_b, w_proj, (((1,), (1,)), ((), ())), preferred_element_type=jnp.float32
    )
    _, pull_norm = jax.vjp(lambda v: layer_norm(v, final_gain), out)
    (dout,) = pull_norm(dfinal)
    dout_b = dout.astype(jnp.bfloat16)
    group_grad = lax.all_gather(dout_b, "grp", axis=0, tiled=True)
    dhid = jnp.dot(group_grad, w_down_t, preferred_element_type=jnp.float32)
    dgate = (dhid * up * gelu_slope(gate)).astype(jnp.bfloat16)
    dup = (dhid * gelu_exact(gate)).astype(jnp.bfloat16)
    term_gate = lax.dot_general(group_rows, dgate, contract, preferred_element_type=jnp.float32)
    term_up = lax.dot_general(group_rows, dup, contract, preferred_element_type=jnp.float32)
    term_down = lax.dot_general(group_grad, hidden, contract, preferred_element_type=jnp.float32)
    grad_gate, grad_up, grad_down, grad_proj = scatter_sums(
        term_gate.astype(jnp.bfloat16),
        term_up.astype(jnp.bfloat16),
        term_down.astype(jnp.bfloat16),
        proj_term,
        side,
    )
    return (losses, grad_gate, grad_up, grad_down, grad_proj)


def solution(mesh):
    placed = (
        P(("shard", "grp"), None, None),
        P(),
        P(),
        P(None, "grp"),
        P(None, "grp"),
        P(None, "grp"),
        P(),
        P("grp", None),
        P(None, "grp"),
        P("shard", None),
        P("shard", "grp", None),
        P(),
        P(("shard", "grp"), None),
    )
    return jax.shard_map(
        local,
        mesh=mesh,
        in_specs=placed,
        out_specs=(
            P(("shard", "grp")),
            P("shard", "grp"),
            P("shard", "grp"),
            P("shard", "grp"),
            P(("shard", "grp"), None),
        ),
        check_vma=False,
    )
```

```python
import functools
import math

import jax
import jax.numpy as jnp
from jax import lax
from jax.experimental import pallas as pl
from jax.experimental.pallas import tpu as pltpu
from jax.sharding import PartitionSpec as P

MESH = pl.DeviceIdType.MESH


def layer_norm(rows, gain):
    centre = rows - jnp.mean(rows, axis=-1, keepdims=True)
    spread = jnp.mean(centre * centre, axis=-1, keepdims=True)
    return centre * lax.rsqrt(spread + 1e-05) * gain


def rebuild_passage(p, blk_ref, lane_ref, codes_ref, bucket_ref, tab):
    dims, toks = tab.shape[0], lane_ref.shape[1]
    lane = lax.broadcasted_iota(jnp.int32, (dims, toks), 1)
    shift = 2 * lax.broadcasted_iota(jnp.int32, (8, toks), 0)
    spot = jnp.broadcast_to(lane_ref[pl.ds(p, 1), :], (dims, toks))
    base = jnp.zeros((dims, toks), jnp.float32)
    for j in range(toks):
        block = tab[:, pl.ds(blk_ref[p, j] * 128, 128)].astype(jnp.float32)
        base = jnp.where(lane == j, jnp.take_along_axis(block, spot, axis=1), base)
    words = codes_ref[p]
    fields = jnp.concatenate(
        [
            jnp.bitwise_and(
                jnp.right_shift(jnp.broadcast_to(words[w : w + 1], (8, toks)), shift), 3
            )
            for w in range(dims // 8)
        ],
        axis=0,
    )
    resid = jnp.where(
        fields < 2,
        jnp.where(fields == 0, bucket_ref[0], bucket_ref[1]),
        jnp.where(fields == 2, bucket_ref[2], bucket_ref[3]),
    )
    return (base + resid).astype(jnp.bfloat16)


def pair(docs, queries, count):
    q_len, dim = queries.shape
    toks = docs.shape[1]
    spots = lax.broadcasted_iota(jnp.int32, (q_len, toks), 1)
    values = docs.astype(jnp.float32)
    scale = lax.rsqrt(jnp.mean(values * values, axis=0, keepdims=True) + 1e-06) / math.sqrt(dim)
    sims = jnp.dot(queries, docs, preferred_element_type=jnp.float32)
    raised = jnp.where(spots < count, jnp.exp(64.0 * (sims * scale)), 0.0)
    total = jnp.sum(raised, axis=1, keepdims=True)
    score = jnp.sum(jnp.log(total), axis=0, keepdims=True) / 64.0
    weights = (raised * (scale / total)).astype(jnp.bfloat16)
    pull = lax.dot_general(
        weights, docs, (((1,), (1,)), ((), ())), preferred_element_type=jnp.float32
    )
    return pull.astype(jnp.bfloat16), score


def forward_kernel(
    side, groups, chunks,
    states_ref, norm_gain_ref, final_gain_ref, gate_w, up_w, down_w, proj_w,
    blk_ref, lens_ref, lane_ref, codes_ref, bucket_ref, tables_ref, tab_hbm,
    rows_ref, slope_ref, gelu_ref, hidden_ref, out_ref, final_ref, proj_ref, pull_ref, score_ref,
    tab, docs, part, part_own, part_land, asks, asks_smem, queries, pull_out, score_out,
    tab_sem, asks_sem, rows_send, rows_recv, part_send, part_recv, docs_send, docs_recv,
    asks_send, asks_recv, query_send, query_recv, pull_send, pull_recv, score_send, score_recv,
):
    z, x, core, grp = coords(side)
    me = (z * side + x) * 2 + core
    shards = 2 * side * side
    passages, toks = lane_ref.shape
    span = passages // chunks
    tok_rows = states_ref.shape[0]
    caps, q_len, dim = pull_ref.shape[1:]

    pieces = tab_sem.shape[0]
    width = tab.shape[1] // pieces
    table_copies = [
        pltpu.make_async_copy(
            tab_hbm.at[:, pl.ds(i * width, width)], tab.at[:, pl.ds(i * width, width)], tab_sem.at[i]
        )
        for i in range(pieces)
    ]
    for copy in table_copies:
        copy.start()

    def to(step):
        dz, dx, dc = step // (2 * side), (step // 2) % side, step % 2
        return (((z + dz) % side) * side + (x + dx) % side) * 2 + (core + dc) % 2

    def source(step):
        dz, dx, dc = step // (2 * side), (step // 2) % side, step % 2
        return (
            ((z + side - dz) % side) * side + (x + side - dx) % side
        ) * 2 + (core + 2 - dc) % 2

    barrier = pltpu.get_barrier_semaphore()

    def greet(step, carry):
        pl.semaphore_signal(barrier, inc=1, device_id=(to(step), grp), device_id_type=MESH)
        return carry

    lax.fori_loop(1, shards, greet, 0)
    for step in range(1, groups):
        pl.semaphore_signal(
            barrier, inc=1, device_id=(me, (grp + step) % groups), device_id_type=MESH
        )
    rows_ref[grp] = layer_norm(states_ref[...].astype(jnp.float32), norm_gain_ref[...]).astype(
        jnp.bfloat16
    )
    pl.semaphore_wait(barrier, shards + groups - 2)

    def along_grp(step, src, dst, send_sem, recv_sem):
        return pltpu.make_async_remote_copy(
            src_ref=src, dst_ref=dst, send_sem=send_sem, recv_sem=recv_sem,
            device_id=(me, (grp + step) % groups), device_id_type=MESH,
        )

    def came(step):
        return (grp + groups - step) % groups

    def rows_copy(step, slot):
        return along_grp(
            step, rows_ref.at[slot], rows_ref.at[slot], rows_send.at[step], rows_recv.at[step]
        )

    def part_copy(step):
        return along_grp(
            step, part.at[(grp + step) % groups], part_land.at[step - 1],
            part_send.at[step], part_recv.at[step],
        )

    def docs_copy(step, chunk, slot):
        place = docs.at[slot, pl.ds(chunk * span, span)]
        return along_grp(
            step, place, place, docs_send.at[chunk, step], docs_recv.at[chunk, step]
        )

    def along_shard(step, src, dst, send_sems, recv_sems):
        return pltpu.make_async_remote_copy(
            src_ref=src, dst_ref=dst, send_sem=send_sems.at[step], recv_sem=recv_sems.at[step],
            device_id=(to(step), grp), device_id_type=MESH,
        )

    def asks_copy(step, slot):
        return along_shard(step, tables_ref.at[to(step)], asks.at[slot], asks_send, asks_recv)

    def query_copy(step, slot):
        return along_shard(step, queries.at[me], queries.at[slot], query_send, query_recv)

    def back(step, src, dst, send_sems, recv_sems):
        return pltpu.make_async_remote_copy(
            src_ref=src, dst_ref=dst, send_sem=send_sems.at[step], recv_sem=recv_sems.at[step],
            device_id=(source(step), grp), device_id_type=MESH,
        )

    def pull_copy(step, slot):
        return back(step, pull_out.at[source(step)], pull_ref.at[slot], pull_send, pull_recv)

    def score_copy(step, slot):
        return back(step, score_out.at[source(step)], score_ref.at[slot], score_send, score_recv)

    for step in range(1, groups):
        rows_copy(step, grp).start()

    def ask(step, carry):
        asks_copy(step, me).start()
        return carry

    lax.fori_loop(1, shards, ask, 0)
    asks[me] = tables_ref[me]
    for copy in table_copies:
        copy.wait()

    def feed_forward():
        for step in range(1, groups):
            rows_copy(step, came(step)).wait_recv()

        def block(r, carry):
            normed = rows_ref[r]
            gate = jnp.dot(normed, gate_w[...], preferred_element_type=jnp.float32)
            up = jnp.dot(normed, up_w[...], preferred_element_type=jnp.float32)
            cdf = 0.5 * (1.0 + lax.erf(gate * (1.0 / math.sqrt(2.0))))
            gelu = gate * cdf
            bell = jnp.exp(-0.5 * gate * gate) * (1.0 / math.sqrt(2.0 * math.pi))
            slope_ref[r] = ((cdf + gate * bell) * up).astype(jnp.bfloat16)
            gelu_ref[r] = gelu.astype(jnp.bfloat16)
            hidden = (gelu * up).astype(jnp.bfloat16)
            hidden_ref[r] = hidden
            down = lax.dot_general(
                hidden, down_w[...], (((1,), (1,)), ((), ())), preferred_element_type=jnp.float32
            )
            part[r] = down.astype(jnp.bfloat16)

            @pl.when(r == grp)
            def _():
                part_own[...] = down

            return carry

        lax.fori_loop(0, groups, block, 0)
        for step in range(1, groups):
            part_copy(step).start()

    def make_queries():
        out = states_ref[...].astype(jnp.float32) + part_own[...]
        for step in range(1, groups):
            part_copy(step).wait_recv()
            out = out + part_land[step - 1].astype(jnp.float32)
        out_ref[...] = out
        final = layer_norm(out, final_gain_ref[...]).astype(jnp.bfloat16)
        final_ref[...] = final
        proj = jnp.dot(final, proj_w[...], preferred_element_type=jnp.float32)
        proj_ref[...] = proj
        scale = lax.rsqrt(jnp.mean(proj * proj, axis=-1, keepdims=True) + 1e-06) / math.sqrt(dim)
        queries[me] = (proj * scale).astype(jnp.bfloat16).reshape(tok_rows // q_len, q_len, dim)

        def tell(step, carry):
            query_copy(step, me).start()
            return carry

        lax.fori_loop(1, shards, tell, 0)

    def chunk_of(c, carry):
        def passage(i, carry):
            p = c * span + i
            docs[grp, p] = rebuild_passage(p, blk_ref, lane_ref, codes_ref, bucket_ref, tab)
            return carry

        lax.fori_loop(0, span, passage, 0)
        for step in range(1, groups):
            docs_copy(step, c, grp).start()
        pl.when(c == 0)(feed_forward)
        pl.when(c == chunks // 2)(make_queries)
        return carry

    lax.fori_loop(0, chunks, chunk_of, 0)

    def gather_in(step, carry):
        asks_copy(step, source(step)).wait_recv()
        query_copy(step, source(step)).wait_recv()
        return carry

    lax.fori_loop(1, shards, gather_in, 0)
    to_smem = pltpu.make_async_copy(asks, asks_smem, asks_sem)
    to_smem.start()
    to_smem.wait()

    def docs_in(c, carry):
        for step in range(1, groups):
            docs_copy(step, c, came(step)).wait_recv()
        return carry

    lax.fori_loop(0, chunks, docs_in, 0)

    def serve(step, carry):
        d = source(step)
        for k in range(caps):
            p = asks_smem[d, 0, k]
            raw = jnp.concatenate([docs[g, p] for g in range(groups)], axis=0)
            pull, score = pair(raw, queries[d, asks_smem[d, 0, caps + k]], lens_ref[p])
            pull_out[d, k] = pull
            score_out[d, pl.ds(k, 1), :] = jnp.broadcast_to(score, (1, dim))

        @pl.when(step > 0)
        def _():
            pull_copy(step, me).start()
            score_copy(step, me).start()

        @pl.when(step == 0)
        def _():
            pull_ref[me] = pull_out[me]
            score_ref[me] = score_out[me]

        return carry

    lax.fori_loop(0, shards, serve, 0)

    def finish(step, carry):
        pull_copy(step, to(step)).wait_recv()
        score_copy(step, to(step)).wait_recv()
        asks_copy(step, me).wait_send()
        query_copy(step, me).wait_send()
        pull_copy(step, me).wait_send()
        score_copy(step, me).wait_send()
        return carry

    lax.fori_loop(1, shards, finish, 0)
    for step in range(1, groups):
        rows_copy(step, grp).wait_send()
        part_copy(step).wait_send()

    def docs_out(c, carry):
        for step in range(1, groups):
            docs_copy(step, c, grp).wait_send()
        return carry

    lax.fori_loop(0, chunks, docs_out, 0)


def forward(
    states, norm_gain, final_gain, w_gate, w_up, w_down_t, w_proj, cent_ids, lens, codes, bucket,
    tables, table, side, caps, q_len,
):
    groups = lax.axis_size("grp")
    shards = 2 * side * side
    tok_rows, width = states.shape
    part = w_gate.shape[1]
    dim = w_proj.shape[1]
    passages, toks = cent_ids.shape
    dims, count = table.shape
    chunks = 8
    spread = jnp.broadcast_to(bucket[:, :, None], (4, dims, toks))
    vmem = pl.BlockSpec(memory_space=pltpu.VMEM)
    smem = pl.BlockSpec(memory_space=pltpu.SMEM)
    bf16, f32 = jnp.bfloat16, jnp.float32
    dma = pltpu.SemaphoreType.DMA
    return pl.pallas_call(
        functools.partial(forward_kernel, side, groups, chunks),
        out_shape=(
            jax.ShapeDtypeStruct((groups, tok_rows, width), bf16),
            jax.ShapeDtypeStruct((groups, tok_rows, part), bf16),
            jax.ShapeDtypeStruct((groups, tok_rows, part), bf16),
            jax.ShapeDtypeStruct((groups, tok_rows, part), bf16),
            jax.ShapeDtypeStruct((tok_rows, width), f32),
            jax.ShapeDtypeStruct((tok_rows, width), bf16),
            jax.ShapeDtypeStruct((tok_rows, dim), f32),
            jax.ShapeDtypeStruct((shards, caps, q_len, dim), bf16),
            jax.ShapeDtypeStruct((shards, caps, dim), f32),
        ),
        in_specs=[vmem] * 7 + [smem] * 2 + [vmem] * 4 + [pl.BlockSpec(memory_space=pl.ANY)],
        out_specs=(vmem,) * 9,
        scratch_shapes=[
            pltpu.VMEM((dims, count), bf16),
            pltpu.VMEM((groups, passages, dims, toks), bf16),
            pltpu.VMEM((groups, tok_rows, width), bf16),
            pltpu.VMEM((tok_rows, width), f32),
            pltpu.VMEM((groups - 1, tok_rows, width), bf16),
            pltpu.VMEM((shards, 1, 128), jnp.int32),
            pltpu.SMEM((shards, 1, 128), jnp.int32),
            pltpu.VMEM((shards, tok_rows // q_len, q_len, dim), bf16),
            pltpu.VMEM((shards, caps, q_len, dim), bf16),
            pltpu.VMEM((shards, caps, dim), f32),
            dma((8,)),
            dma,
        ]
        + [dma((groups,))] * 4
        + [dma((chunks, groups))] * 2
        + [dma((shards,))] * 8,
        compiler_params=pltpu.CompilerParams(
            collective_id=1, has_side_effects=True, vmem_limit_bytes=56 << 20
        ),
        cost_estimate=pl.CostEstimate(flops=0, bytes_accessed=300_000_000, transcendentals=0),
    )(
        states, norm_gain, final_gain, w_gate, w_up, w_down_t, w_proj, cent_ids >> 7, lens,
        cent_ids & 127, codes, spread, tables, table,
    )


def coords(shape):
    me = lax.axis_index("shard")
    return me // (2 * shape), (me // 2) % shape, me % 2, lax.axis_index("grp")


def scatter_kernel(
    side, groups, gate_ref, up_ref, down_ref, proj_ref, gate_out, up_out, down_out, proj_out,
    twin, twin_proj, held, held_proj, land, land_proj, rows_sum, land_grp,
    twin_send, twin_recv, chip_send, chip_recv, grp_send, grp_recv,
):
    z, x, core, grp = coords(side)
    chips = side * side
    chip = z * side + x
    sibling = (chip * 2 + 1 - core, grp)

    def peer(step):
        other = ((z + step // side) % side) * side + (x + step % side) % side
        return other, (other * 2 + core, grp)

    barrier = pltpu.get_barrier_semaphore()
    pl.semaphore_signal(barrier, inc=1, device_id=sibling, device_id_type=MESH)
    for step in range(1, chips):
        pl.semaphore_signal(barrier, inc=1, device_id=peer(step)[1], device_id_type=MESH)
    for step in range(1, groups):
        pl.semaphore_signal(
            barrier, inc=1, device_id=(chip * 2 + core, (grp + step) % groups), device_id_type=MESH
        )
    pl.semaphore_wait(barrier, chips + groups - 1)

    terms = (gate_ref, up_ref, down_ref)

    def swap(src, dst, i):
        return pltpu.make_async_remote_copy(
            src_ref=src, dst_ref=dst, send_sem=twin_send.at[i], recv_sem=twin_recv.at[i],
            device_id=sibling, device_id_type=MESH,
        )

    first = [swap(proj_ref.at[:, 1 - core], twin_proj, 3)]
    first += [swap(terms[i].at[:, 1 - core], twin.at[:, i], i) for i in range(3)]
    for copy in first:
        copy.start()
    first[0].wait_recv()

    def add_proj(c, carry):
        held_proj[c] = proj_ref[c, core] + twin_proj[c]
        return carry

    lax.fori_loop(0, chips, add_proj, 0)
    for i in range(3):
        first[1 + i].wait_recv()

        def add(c, carry):
            held[c, i] = (
                terms[i][c, core].astype(jnp.float32) + twin[c, i].astype(jnp.float32)
            ).astype(jnp.bfloat16)
            return carry

        lax.fori_loop(0, chips, add, 0)

    def send(step, src, dst, kind):
        other, device = peer(step)
        return pltpu.make_async_remote_copy(
            src_ref=src.at[other], dst_ref=dst.at[step - 1],
            send_sem=chip_send.at[kind, step - 1], recv_sem=chip_recv.at[kind, step - 1],
            device_id=device, device_id_type=MESH,
        )

    small = [send(step, held_proj, land_proj, 0) for step in range(1, chips)]
    large = [send(step, held, land, 1) for step in range(1, chips)]
    for copy in small:
        copy.start()
    for copy in large:
        copy.start()
    for copy in small:
        copy.wait_recv()
    total = held_proj[chip]
    for step in range(1, chips):
        total = total + land_proj[step - 1]
    rows_sum[...] = total.reshape(rows_sum.shape)
    last = []
    for step in range(1, groups):
        other = (grp + step) % groups
        last.append(
            pltpu.make_async_remote_copy(
                src_ref=rows_sum.at[other], dst_ref=land_grp.at[step - 1],
                send_sem=grp_send.at[step - 1], recv_sem=grp_recv.at[step - 1],
                device_id=(chip * 2 + core, other), device_id_type=MESH,
            )
        )
        last[-1].start()
    for copy in last:
        copy.wait_recv()
    mine = rows_sum[grp]
    for step in range(1, groups):
        mine = mine + land_grp[step - 1]
    proj_out[...] = mine
    for copy in large:
        copy.wait_recv()
    for i, out in enumerate((gate_out, up_out, down_out)):
        total = held[chip, i].astype(jnp.float32)
        for step in range(1, chips):
            total = total + land[step - 1, i].astype(jnp.float32)
        out[...] = total
    for copy in first + small + large + last:
        copy.wait_send()


def scatter_sums(term_gate, term_up, term_down, proj_term, side):
    groups = lax.axis_size("grp")
    width, part = term_gate.shape
    dim = proj_term.shape[1]
    chips = side * side
    rows = width // (2 * chips)
    terms = [t.reshape(chips, 2, rows, part) for t in (term_gate, term_up, term_down)]
    wide = (chips, 3, rows, part)
    return pl.pallas_call(
        functools.partial(scatter_kernel, side, groups),
        out_shape=(jax.ShapeDtypeStruct((rows, part), jnp.float32),) * 3
        + (jax.ShapeDtypeStruct((rows // groups, dim), jnp.float32),),
        in_specs=[pl.BlockSpec(memory_space=pltpu.VMEM)] * 4,
        out_specs=(pl.BlockSpec(memory_space=pltpu.VMEM),) * 4,
        scratch_shapes=[
            pltpu.VMEM(wide, jnp.bfloat16),
            pltpu.VMEM((chips, rows, dim), jnp.float32),
            pltpu.VMEM(wide, jnp.bfloat16),
            pltpu.VMEM((chips, rows, dim), jnp.float32),
            pltpu.VMEM((chips - 1, 3, rows, part), jnp.bfloat16),
            pltpu.VMEM((chips - 1, rows, dim), jnp.float32),
            pltpu.VMEM((groups, rows // groups, dim), jnp.float32),
            pltpu.VMEM((groups - 1, rows // groups, dim), jnp.float32),
            pltpu.SemaphoreType.DMA((4,)),
            pltpu.SemaphoreType.DMA((4,)),
            pltpu.SemaphoreType.DMA((2, chips - 1)),
            pltpu.SemaphoreType.DMA((2, chips - 1)),
            pltpu.SemaphoreType.DMA((groups - 1,)),
            pltpu.SemaphoreType.DMA((groups - 1,)),
        ],
        compiler_params=pltpu.CompilerParams(
            collective_id=0, has_side_effects=True, vmem_limit_bytes=32 << 20
        ),
        cost_estimate=pl.CostEstimate(flops=0, bytes_accessed=60_000_000, transcendentals=0),
    )(*terms, proj_term.reshape(chips, 2, rows, dim))


def ranks(hits):
    count = hits.shape[1]
    before = lax.broadcasted_iota(jnp.int32, (count, count), 0) < lax.broadcasted_iota(
        jnp.int32, (count, count), 1
    )
    return jnp.dot(
        hits.astype(jnp.bfloat16), before.astype(jnp.bfloat16), preferred_element_type=jnp.float32
    ).astype(jnp.int32)


def slots(hits, caps):
    nth = lax.broadcasted_iota(jnp.int32, (1, caps, 1), 1)
    return hits[:, None, :] & (ranks(hits)[:, None, :] == nth)


def local(
    query_states,
    norm_gain,
    final_gain,
    w_gate,
    w_up,
    w_down_t,
    w_proj,
    centroids,
    bucket_values,
    centroid_ids,
    residual_codes,
    passage_lens,
    negative_ids,
):
    q_dev, q_len, width = query_states.shape
    dim = w_proj.shape[1]
    shards = lax.axis_size("shard")
    groups = lax.axis_size("grp")
    side = math.isqrt(shards // 2)
    cands = negative_ids.shape[1]
    tok_rows = q_dev * q_len
    local_pass = centroid_ids.shape[0]
    caps = 2 * q_dev * cands // shards
    me = lax.axis_index("shard")

    flat_ids = negative_ids.reshape(1, -1)
    owner = lax.broadcasted_iota(jnp.int32, (shards, 1), 0)
    places = lax.broadcasted_iota(jnp.int32, (1, 1, q_dev * cands), 2)
    sent = slots(flat_ids // local_pass == owner, caps)
    place = jnp.sum(jnp.where(sent, places, 0), axis=2)
    asked = jnp.sum(jnp.where(sent, (flat_ids % local_pass)[:, None, :], 0), axis=2)
    tables = jnp.concatenate(
        [asked, place // cands, jnp.zeros((shards, 128 - 2 * caps), jnp.int32)], axis=1
    ).reshape(shards, 1, 128)
    lens = lax.dynamic_slice(passage_lens, (me * local_pass,), (local_pass,))
    states = query_states.reshape(tok_rows, width)
    group_rows, slope, gelu, hidden, out, final, proj, pull, score = forward(
        states, norm_gain.reshape(1, -1), final_gain.reshape(1, -1), w_gate, w_up, w_down_t, w_proj,
        centroid_ids, lens, residual_codes, bucket_values, tables, centroids, side, caps, q_len,
    )
    group_rows = group_rows.reshape(groups * tok_rows, width)
    slope, gelu, hidden = (v.reshape(groups * tok_rows, -1) for v in (slope, gelu, hidden))
    length = lax.rsqrt(jnp.mean(proj * proj, axis=-1, keepdims=True) + 1e-06)
    scale = length / math.sqrt(dim)

    filled = jnp.any(sent, axis=2).reshape(1, -1)
    place = place.reshape(1, -1)
    query = lax.broadcasted_iota(jnp.int32, (q_dev, 1), 0)
    mine = filled & (place // cands == query)
    first = mine & (place % cands == 0)
    scores = 10.0 * score[:, :, 0].reshape(1, -1)
    top = jnp.max(jnp.where(mine, scores, -jnp.inf), axis=1, keepdims=True)
    raised = jnp.where(mine, jnp.exp(scores - top), 0.0)
    total = jnp.sum(raised, axis=1, keepdims=True)
    losses = (
        top + jnp.log(total) - jnp.sum(jnp.where(first, scores, 0.0), axis=1, keepdims=True)
    ).reshape(q_dev)
    weights = 10.0 * (raised / total - first.astype(jnp.float32))
    high = weights.astype(jnp.bfloat16)
    low = (weights - high.astype(jnp.float32)).astype(jnp.bfloat16)
    both = jnp.dot(
        jnp.concatenate([high, low], axis=0),
        pull.reshape(shards * caps, q_len * dim),
        preferred_element_type=jnp.float32,
    )
    dqueries = (both[:q_dev] + both[q_dev:]).reshape(tok_rows, dim)
    dqueries = dqueries.astype(jnp.bfloat16).astype(jnp.float32)
    along = jnp.mean(dqueries * proj, axis=-1, keepdims=True)
    dproj_b = (scale * (dqueries - proj * (length * length * along))).astype(jnp.bfloat16)

    contract = (((0,), (0,)), ((), ()))
    proj_term = lax.dot_general(final, dproj_b, contract, preferred_element_type=jnp.float32)
    dfinal = lax.dot_general(
        dproj_b, w_proj, (((1,), (1,)), ((), ())), preferred_element_type=jnp.float32
    )
    _, pull_norm = jax.vjp(lambda v: layer_norm(v, final_gain), out)
    (dout,) = pull_norm(dfinal)
    dout_b = dout.astype(jnp.bfloat16)
    group_grad = lax.all_gather(dout_b, "grp", axis=0, tiled=True)
    dhid = jnp.dot(group_grad, w_down_t, preferred_element_type=jnp.float32)
    dgate = (dhid * slope.astype(jnp.float32)).astype(jnp.bfloat16)
    dup = (dhid * gelu.astype(jnp.float32)).astype(jnp.bfloat16)
    term_gate = lax.dot_general(group_rows, dgate, contract, preferred_element_type=jnp.float32)
    term_up = lax.dot_general(group_rows, dup, contract, preferred_element_type=jnp.float32)
    term_down = lax.dot_general(group_grad, hidden, contract, preferred_element_type=jnp.float32)
    grad_gate, grad_up, grad_down, grad_proj = scatter_sums(
        term_gate.astype(jnp.bfloat16),
        term_up.astype(jnp.bfloat16),
        term_down.astype(jnp.bfloat16),
        proj_term,
        side,
    )
    return (losses, grad_gate, grad_up, grad_down, grad_proj)


def solution(mesh):
    placed = (
        P(("shard", "grp"), None, None),
        P(),
        P(),
        P(None, "grp"),
        P(None, "grp"),
        P(None, "grp"),
        P(),
        P("grp", None),
        P(None, "grp"),
        P("shard", None),
        P("shard", "grp", None),
        P(),
        P(("shard", "grp"), None),
    )
    return jax.shard_map(
        local,
        mesh=mesh,
        in_specs=placed,
        out_specs=(
            P(("shard", "grp")),
            P("shard", "grp"),
            P("shard", "grp"),
            P("shard", "grp"),
            P(("shard", "grp"), None),
        ),
        check_vma=False,
    )
```

```python
import functools
import math

import jax
import jax.numpy as jnp
from jax import lax
from jax.experimental import pallas as pl
from jax.experimental.pallas import tpu as pltpu
from jax.sharding import PartitionSpec as P

MESH = pl.DeviceIdType.MESH


def layer_norm(rows, gain):
    centre = rows - jnp.mean(rows, axis=-1, keepdims=True)
    spread = jnp.mean(centre * centre, axis=-1, keepdims=True)
    return centre * lax.rsqrt(spread + 1e-05) * gain


def rebuild_passage(p, blk_ref, lane_ref, codes_ref, bucket_ref, tab):
    dims, toks = tab.shape[0], lane_ref.shape[1]
    lane = lax.broadcasted_iota(jnp.int32, (dims, toks), 1)
    shift = 2 * lax.broadcasted_iota(jnp.int32, (8, toks), 0)
    spot = jnp.broadcast_to(lane_ref[pl.ds(p, 1), :], (dims, toks))
    base = jnp.zeros((dims, toks), jnp.float32)
    for j in range(toks):
        block = tab[:, pl.ds(blk_ref[p, j] * 128, 128)].astype(jnp.float32)
        base = jnp.where(lane == j, jnp.take_along_axis(block, spot, axis=1), base)
    words = codes_ref[p]
    fields = jnp.concatenate(
        [
            jnp.bitwise_and(
                jnp.right_shift(jnp.broadcast_to(words[w : w + 1], (8, toks)), shift), 3
            )
            for w in range(dims // 8)
        ],
        axis=0,
    )
    resid = jnp.where(
        fields < 2,
        jnp.where(fields == 0, bucket_ref[0], bucket_ref[1]),
        jnp.where(fields == 2, bucket_ref[2], bucket_ref[3]),
    )
    return (base + resid).astype(jnp.bfloat16)


def dot_t(left, right):
    return lax.dot_general(
        left, right, (((1,), (1,)), ((), ())), preferred_element_type=jnp.float32
    )


def pair(docs, queries, count):
    q_len, dim = queries.shape
    toks = docs.shape[1]
    spots = lax.broadcasted_iota(jnp.int32, (q_len, toks), 1)
    values = docs.astype(jnp.float32)
    scale = lax.rsqrt(jnp.mean(values * values, axis=0, keepdims=True) + 1e-06) / math.sqrt(dim)
    sims = jnp.dot(queries, docs, preferred_element_type=jnp.float32)
    raised = jnp.where(spots < count, jnp.exp(64.0 * (sims * scale)), 0.0)
    total = jnp.sum(raised, axis=1, keepdims=True)
    score = jnp.sum(jnp.log(total), axis=0, keepdims=True) / 64.0
    pull = dot_t((raised * (scale / total)).astype(jnp.bfloat16), docs)
    return pull.astype(jnp.bfloat16), score


def step_kernel(
    side, groups, chunks,
    states_ref, norm_gain_ref, final_gain_ref, gate_w, up_w, down_w, proj_w,
    blk_ref, lens_ref, lane_ref, codes_ref, bucket_ref, tables_ref, which_ref, tab_hbm,
    loss_ref, gate_out, up_out, down_out, proj_out,
    tab, docs, rows_ref, slope_ref, gelu_ref, hidden_ref, part, part_own, part_land, out_ref,
    final_t, proj_ref, asks, asks_smem, queries, pull_out, score_out, pull_ref, score_ref,
    weights, douts, rows_t, douts_t, dgate, dup, first, twin, held, land,
    proj_term, twin_proj, held_proj, land_proj, rows_sum, land_grp,
    tab_sem, asks_sem, rows_send, rows_recv, part_send, part_recv, dout_send, dout_recv,
    grp_send, grp_recv, docs_send, docs_recv,
    asks_send, asks_recv, query_send, query_recv, pull_send, pull_recv, score_send, score_recv,
    twin_send, twin_recv, chip_send, chip_recv,
):
    z, x, core, grp = coords(side)
    me = (z * side + x) * 2 + core
    shards = 2 * side * side
    passages, toks = lane_ref.shape
    span = passages // chunks
    tok_rows = states_ref.shape[0]
    caps, q_len, dim = pull_ref.shape[1:]

    pieces = tab_sem.shape[0]
    width = tab.shape[1] // pieces
    table_copies = [
        pltpu.make_async_copy(
            tab_hbm.at[:, pl.ds(i * width, width)], tab.at[:, pl.ds(i * width, width)], tab_sem.at[i]
        )
        for i in range(pieces)
    ]
    for copy in table_copies:
        copy.start()

    def to(step):
        dz, dx, dc = step // (2 * side), (step // 2) % side, step % 2
        return (((z + dz) % side) * side + (x + dx) % side) * 2 + (core + dc) % 2

    def source(step):
        dz, dx, dc = step // (2 * side), (step // 2) % side, step % 2
        return (
            ((z + side - dz) % side) * side + (x + side - dx) % side
        ) * 2 + (core + 2 - dc) % 2

    barrier = pltpu.get_barrier_semaphore()

    def greet(step, carry):
        pl.semaphore_signal(barrier, inc=1, device_id=(to(step), grp), device_id_type=MESH)
        return carry

    lax.fori_loop(1, shards, greet, 0)
    for step in range(1, groups):
        pl.semaphore_signal(
            barrier, inc=1, device_id=(me, (grp + step) % groups), device_id_type=MESH
        )
    rows_ref[grp] = layer_norm(states_ref[...].astype(jnp.float32), norm_gain_ref[...]).astype(
        jnp.bfloat16
    )
    pl.semaphore_wait(barrier, shards + groups - 2)

    def along_grp(step, src, dst, send_sem, recv_sem):
        return pltpu.make_async_remote_copy(
            src_ref=src, dst_ref=dst, send_sem=send_sem, recv_sem=recv_sem,
            device_id=(me, (grp + step) % groups), device_id_type=MESH,
        )

    def came(step):
        return (grp + groups - step) % groups

    def rows_copy(step, slot):
        return along_grp(
            step, rows_ref.at[slot], rows_ref.at[slot], rows_send.at[step], rows_recv.at[step]
        )

    def part_copy(step):
        return along_grp(
            step, part.at[(grp + step) % groups], part_land.at[step - 1],
            part_send.at[step], part_recv.at[step],
        )

    def docs_copy(step, chunk, slot):
        place = docs.at[slot, pl.ds(chunk * span, span)]
        return along_grp(
            step, place, place, docs_send.at[chunk, step], docs_recv.at[chunk, step]
        )

    def along_shard(step, src, dst, send_sems, recv_sems):
        return pltpu.make_async_remote_copy(
            src_ref=src, dst_ref=dst, send_sem=send_sems.at[step], recv_sem=recv_sems.at[step],
            device_id=(to(step), grp), device_id_type=MESH,
        )

    def asks_copy(step, slot):
        return along_shard(step, tables_ref.at[to(step)], asks.at[slot], asks_send, asks_recv)

    def query_copy(step, slot):
        return along_shard(step, queries.at[me], queries.at[slot], query_send, query_recv)

    def back(step, src, dst, send_sems, recv_sems):
        return pltpu.make_async_remote_copy(
            src_ref=src, dst_ref=dst, send_sem=send_sems.at[step], recv_sem=recv_sems.at[step],
            device_id=(source(step), grp), device_id_type=MESH,
        )

    def pull_copy(step, slot):
        return back(step, pull_out.at[source(step)], pull_ref.at[slot], pull_send, pull_recv)

    def score_copy(step, slot):
        return back(step, score_out.at[source(step)], score_ref.at[slot], score_send, score_recv)

    for step in range(1, groups):
        rows_copy(step, grp).start()

    def ask(step, carry):
        asks_copy(step, me).start()
        return carry

    lax.fori_loop(1, shards, ask, 0)
    asks[me] = tables_ref[me]
    for copy in table_copies:
        copy.wait()

    def feed_forward():
        for step in range(1, groups):
            rows_copy(step, came(step)).wait_recv()

        def block(r, carry):
            normed = rows_ref[r]
            gate = dot_t(normed, gate_w[...])
            up = dot_t(normed, up_w[...])
            cdf = 0.5 * (1.0 + lax.erf(gate * (1.0 / math.sqrt(2.0))))
            gelu = gate * cdf
            bell = jnp.exp(-0.5 * gate * gate) * (1.0 / math.sqrt(2.0 * math.pi))
            slope_ref[r] = ((cdf + gate * bell) * up).astype(jnp.bfloat16)
            gelu_ref[r] = gelu.astype(jnp.bfloat16)
            hidden = (gelu * up).astype(jnp.bfloat16)
            hidden_ref[r] = hidden
            down = jnp.dot(hidden, down_w[...], preferred_element_type=jnp.float32)
            part[r] = down.astype(jnp.bfloat16)

            @pl.when(r == grp)
            def _():
                part_own[...] = down

            return carry

        lax.fori_loop(0, groups, block, 0)
        for step in range(1, groups):
            part_copy(step).start()

    def make_queries():
        out = states_ref[...].astype(jnp.float32) + part_own[...]
        for step in range(1, groups):
            part_copy(step).wait_recv()
            out = out + part_land[step - 1].astype(jnp.float32)
        out_ref[...] = out
        final = layer_norm(out, final_gain_ref[...]).astype(jnp.bfloat16)
        final_t[...] = final.T
        proj = jnp.dot(final, proj_w[...], preferred_element_type=jnp.float32)
        proj_ref[...] = proj
        scale = lax.rsqrt(jnp.mean(proj * proj, axis=-1, keepdims=True) + 1e-06) / math.sqrt(dim)
        queries[me] = (proj * scale).astype(jnp.bfloat16).reshape(tok_rows // q_len, q_len, dim)

        def tell(step, carry):
            query_copy(step, me).start()
            return carry

        lax.fori_loop(1, shards, tell, 0)

    def chunk_of(c, carry):
        def passage(i, carry):
            p = c * span + i
            docs[grp, p] = rebuild_passage(p, blk_ref, lane_ref, codes_ref, bucket_ref, tab)
            return carry

        lax.fori_loop(0, span, passage, 0)
        for step in range(1, groups):
            docs_copy(step, c, grp).start()
        pl.when(c == 0)(feed_forward)
        pl.when(c == chunks // 2)(make_queries)
        return carry

    lax.fori_loop(0, chunks, chunk_of, 0)

    def gather_in(step, carry):
        asks_copy(step, source(step)).wait_recv()
        query_copy(step, source(step)).wait_recv()
        return carry

    lax.fori_loop(1, shards, gather_in, 0)
    to_smem = pltpu.make_async_copy(asks, asks_smem, asks_sem)
    to_smem.start()
    to_smem.wait()

    def docs_in(c, carry):
        for step in range(1, groups):
            docs_copy(step, c, came(step)).wait_recv()
        return carry

    lax.fori_loop(0, chunks, docs_in, 0)

    def serve(step, carry):
        d = source(step)
        rows = []
        for k in range(caps):
            p = asks_smem[d, 0, k]
            raw = jnp.concatenate([docs[g, p] for g in range(groups)], axis=0)
            pull, score = pair(raw, queries[d, asks_smem[d, 0, caps + k]], lens_ref[p])
            pull_out[d, k] = pull
            rows.append(jnp.broadcast_to(score, (1, dim)))
        score_out[d] = jnp.concatenate(rows + [jnp.zeros((8 - caps, dim), jnp.float32)], axis=0)

        @pl.when(step > 0)
        def _():
            pull_copy(step, me).start()
            score_copy(step, me).start()

        @pl.when(step == 0)
        def _():
            pull_ref[me] = pull_out[me]
            score_ref[me] = score_out[me]

        return carry

    lax.fori_loop(0, shards, serve, 0)

    for r in range(groups):
        turned = rows_ref[r].T.reshape(side * side, 2, rows_t.shape[2], tok_rows)
        rows_t[:, :, :, r * tok_rows : (r + 1) * tok_rows] = turned

    def finish(step, carry):
        pull_copy(step, to(step)).wait_recv()
        score_copy(step, to(step)).wait_recv()
        return carry

    lax.fori_loop(1, shards, finish, 0)

    which = which_ref[...]
    scores = 10.0 * score_ref[...].reshape(which.shape)
    top = jnp.max(jnp.where(which > 0, scores, -1e30), axis=0, keepdims=True)
    raised = jnp.where(which > 0, jnp.exp(scores - top), 0.0)
    total = jnp.sum(raised, axis=0, keepdims=True)
    chosen = jnp.sum(jnp.where(which == 2, scores, 0.0), axis=0, keepdims=True)
    loss_ref[...] = jnp.broadcast_to(top + jnp.log(total) - chosen, loss_ref.shape)
    spread = 10.0 * (raised / total - jnp.where(which == 2, 1.0, 0.0))
    q_dev = tok_rows // q_len
    for q in range(q_dev):
        weights[q] = jnp.broadcast_to(spread[:, q : q + 1], spread.shape).reshape(
            weights.shape[1:]
        )

    def gather_pull(s, sums):
        sums = list(sums)
        for k in range(caps):
            term = pull_ref[s, k].astype(jnp.float32)
            for q in range(q_dev):
                sums[q] = sums[q] + weights[q, s, k : k + 1, :] * term
        return tuple(sums)

    zero = jnp.zeros((q_len, dim), jnp.float32)
    sums = lax.fori_loop(0, shards, gather_pull, (zero,) * q_dev)
    dqueries = jnp.concatenate(sums, axis=0).astype(jnp.bfloat16).astype(jnp.float32)
    proj = proj_ref[...]
    length = lax.rsqrt(jnp.mean(proj * proj, axis=-1, keepdims=True) + 1e-06)
    along = jnp.mean(dqueries * proj, axis=-1, keepdims=True)
    dproj = (
        (length / math.sqrt(dim)) * (dqueries - proj * (length * length * along))
    ).astype(jnp.bfloat16)

    dfinal = dot_t(dproj, proj_w[...]) * final_gain_ref[...]
    out = out_ref[...]
    centre = out - jnp.mean(out, axis=-1, keepdims=True)
    inverse = lax.rsqrt(jnp.mean(centre * centre, axis=-1, keepdims=True) + 1e-05)
    unit = centre * inverse
    dout = inverse * (
        dfinal
        - jnp.mean(dfinal, axis=-1, keepdims=True)
        - unit * jnp.mean(dfinal * unit, axis=-1, keepdims=True)
    )
    douts[grp] = dout.astype(jnp.bfloat16)

    def dout_copy(step, slot):
        return along_grp(
            step, douts.at[slot], douts.at[slot], dout_send.at[step], dout_recv.at[step]
        )

    for step in range(1, groups):
        dout_copy(step, grp).start()

    chips = side * side
    chip = me // 2
    block = rows_t.shape[2]

    def swap(src, dst, i):
        return pltpu.make_async_remote_copy(
            src_ref=src, dst_ref=dst, send_sem=twin_send.at[i], recv_sem=twin_recv.at[i],
            device_id=(chip * 2 + 1 - core, grp), device_id_type=MESH,
        )

    def chip_to(step):
        return ((z + step // side) % side) * side + (x + step % side) % side

    def chip_copy(step, src, dst, kind):
        return pltpu.make_async_remote_copy(
            src_ref=src.at[chip_to(step)], dst_ref=dst.at[step - 1],
            send_sem=chip_send.at[kind, step - 1], recv_sem=chip_recv.at[kind, step - 1],
            device_id=(chip_to(step) * 2 + core, grp), device_id_type=MESH,
        )

    proj_term[...] = jnp.dot(
        final_t[...], dproj, preferred_element_type=jnp.float32
    ).reshape(proj_term.shape)
    proj_swap = swap(proj_term.at[:, 1 - core], twin_proj, side)
    proj_swap.start()

    def spread_back(i, carry):
        @pl.when(i > 0)
        def _():
            dout_copy(i, (grp + groups - i) % groups).wait_recv()

        r = (grp + groups - i) % groups
        dhid = dot_t(douts[r], down_w[...])
        dgate[r] = (dhid * slope_ref[r].astype(jnp.float32)).astype(jnp.bfloat16)
        dup[r] = (dhid * gelu_ref[r].astype(jnp.float32)).astype(jnp.bfloat16)
        return carry

    lax.fori_loop(0, groups, spread_back, 0)
    for r in range(groups):
        turned = douts[r].T.reshape(chips, 2, block, tok_rows)
        douts_t[:, :, :, r * tok_rows : (r + 1) * tok_rows] = turned

    proj_swap.wait_recv()

    def add_proj(c, carry):
        held_proj[c] = proj_term[c, core] + twin_proj[c]
        return carry

    lax.fori_loop(0, chips, add_proj, 0)

    def send_proj(step, carry):
        chip_copy(step, held_proj, land_proj, 0).start()
        return carry

    lax.fori_loop(1, chips, send_proj, 0)

    tokens = groups * tok_rows

    def term(i, start, half):
        left = (rows_t, rows_t, douts_t)[i]
        right = (dgate, dup, hidden_ref)[i]
        return jnp.dot(
            left[pl.ds(start, side), half].reshape(side * block, tokens),
            right[...].reshape(tokens, right.shape[2]),
            preferred_element_type=jnp.float32,
        ).reshape(side, block, right.shape[2])

    def band(i):
        return ((z + 1 + i) % side) * side

    def swap_copy(i):
        return swap(first.at[pl.ds(band(i), side)], twin.at[pl.ds(band(i), side)], i)

    def give(i, carry):
        for n in range(3):
            first[pl.ds(band(i), side), n] = term(n, band(i), 1 - core).astype(jnp.bfloat16)
        swap_copy(i).start()
        return carry

    lax.fori_loop(0, side, give, 0)

    def keep(i, carry):
        swap_copy(i).wait_recv()
        for n in range(3):
            held[pl.ds(band(i), side), n] = (
                term(n, band(i), core) + twin[pl.ds(band(i), side), n].astype(jnp.float32)
            ).astype(jnp.bfloat16)
        for dx in range(side):
            step = ((1 + i) % side) * side + dx

            @pl.when(step > 0)
            def _():
                chip_copy(step, held, land, 1).start()

        return carry

    lax.fori_loop(0, side, keep, 0)

    def proj_in(step, total):
        chip_copy(step, held_proj, land_proj, 0).wait_recv()
        return total + land_proj[step - 1]

    rows_sum[...] = lax.fori_loop(1, chips, proj_in, held_proj[chip]).reshape(rows_sum.shape)

    def sum_copy(step):
        return along_grp(
            step, rows_sum.at[(grp + step) % groups], land_grp.at[step - 1],
            grp_send.at[step], grp_recv.at[step],
        )

    for step in range(1, groups):
        sum_copy(step).start()
    mine = rows_sum[grp]
    for step in range(1, groups):
        sum_copy(step).wait_recv()
        mine = mine + land_grp[step - 1]
    proj_out[...] = mine

    for n, ref in enumerate((gate_out, up_out, down_out)):
        ref[...] = held[chip, n].astype(jnp.float32)

    def sum_in(i, carry):
        for dx in range(side):
            step = ((1 + i) % side) * side + dx

            @pl.when(step > 0)
            def _():
                chip_copy(step, held, land, 1).wait_recv()
                for n, ref in enumerate((gate_out, up_out, down_out)):
                    ref[...] += land[step - 1, n].astype(jnp.float32)

        return carry

    lax.fori_loop(0, side, sum_in, 0)

    def sent(step, carry):
        asks_copy(step, me).wait_send()
        query_copy(step, me).wait_send()
        pull_copy(step, me).wait_send()
        score_copy(step, me).wait_send()
        return carry

    lax.fori_loop(1, shards, sent, 0)
    for step in range(1, groups):
        rows_copy(step, grp).wait_send()
        part_copy(step).wait_send()
        dout_copy(step, grp).wait_send()
        sum_copy(step).wait_send()

    def docs_out(c, carry):
        for step in range(1, groups):
            docs_copy(step, c, grp).wait_send()
        return carry

    lax.fori_loop(0, chunks, docs_out, 0)
    proj_swap.wait_send()

    def swapped(i, carry):
        swap_copy(i).wait_send()
        return carry

    lax.fori_loop(0, side, swapped, 0)

    def chips_out(step, carry):
        chip_copy(step, held_proj, land_proj, 0).wait_send()
        chip_copy(step, held, land, 1).wait_send()
        return carry

    lax.fori_loop(1, chips, chips_out, 0)


def step_call(
    states, norm_gain, final_gain, w_gate, w_up, w_down_t, w_proj, cent_ids, lens, codes, bucket,
    tables, which, table, side, caps, q_len,
):
    groups = lax.axis_size("grp")
    shards = 2 * side * side
    chips = side * side
    tok_rows, width = states.shape
    part = w_gate.shape[0]
    dim = w_proj.shape[1]
    passages, toks = cent_ids.shape
    dims, count = table.shape
    chunks = 8
    block = width // shards
    tokens = groups * tok_rows
    spread = jnp.broadcast_to(bucket[:, :, None], (4, dims, toks))
    vmem = pl.BlockSpec(memory_space=pltpu.VMEM)
    smem = pl.BlockSpec(memory_space=pltpu.SMEM)
    bf16, f32 = jnp.bfloat16, jnp.float32
    dma = pltpu.SemaphoreType.DMA
    wide = (chips, 3, block, part)
    return pl.pallas_call(
        functools.partial(step_kernel, side, groups, chunks),
        out_shape=(jax.ShapeDtypeStruct((8, 128), f32),)
        + (jax.ShapeDtypeStruct((block, part), f32),) * 3
        + (jax.ShapeDtypeStruct((block // groups, dim), f32),),
        in_specs=[vmem] * 7 + [smem] * 2 + [vmem] * 5 + [pl.BlockSpec(memory_space=pl.ANY)],
        out_specs=(vmem,) * 5,
        scratch_shapes=[
            pltpu.VMEM((dims, count), bf16),
            pltpu.VMEM((groups, passages, dims, toks), bf16),
            pltpu.VMEM((groups, tok_rows, width), bf16),
            pltpu.VMEM((groups, tok_rows, part), bf16),
            pltpu.VMEM((groups, tok_rows, part), bf16),
            pltpu.VMEM((groups, tok_rows, part), bf16),
            pltpu.VMEM((groups, tok_rows, width), bf16),
            pltpu.VMEM((tok_rows, width), f32),
            pltpu.VMEM((groups - 1, tok_rows, width), bf16),
            pltpu.VMEM((tok_rows, width), f32),
            pltpu.VMEM((width, tok_rows), bf16),
            pltpu.VMEM((tok_rows, dim), f32),
            pltpu.VMEM((shards, 1, 128), jnp.int32),
            pltpu.SMEM((shards, 1, 128), jnp.int32),
            pltpu.VMEM((shards, tok_rows // q_len, q_len, dim), bf16),
            pltpu.VMEM((shards, caps, q_len, dim), bf16),
            pltpu.VMEM((shards, 8, dim), f32),
            pltpu.VMEM((shards, caps, q_len, dim), bf16),
            pltpu.VMEM((shards, 8, dim), f32),
            pltpu.VMEM((tok_rows // q_len, shards, 8, dim), f32),
            pltpu.VMEM((groups, tok_rows, width), bf16),
            pltpu.VMEM((chips, 2, block, tokens), bf16),
            pltpu.VMEM((chips, 2, block, tokens), bf16),
            pltpu.VMEM((groups, tok_rows, part), bf16),
            pltpu.VMEM((groups, tok_rows, part), bf16),
            pltpu.VMEM(wide, bf16),
            pltpu.VMEM(wide, bf16),
            pltpu.VMEM(wide, bf16),
            pltpu.VMEM((chips - 1, 3, block, part), bf16),
            pltpu.VMEM((chips, 2, block, dim), f32),
            pltpu.VMEM((chips, block, dim), f32),
            pltpu.VMEM((chips, block, dim), f32),
            pltpu.VMEM((chips - 1, block, dim), f32),
            pltpu.VMEM((groups, block // groups, dim), f32),
            pltpu.VMEM((groups - 1, block // groups, dim), f32),
            dma((8,)),
            dma,
        ]
        + [dma((groups,))] * 8
        + [dma((chunks, groups))] * 2
        + [dma((shards,))] * 8
        + [dma((side + 1,))] * 2
        + [dma((2, chips - 1))] * 2,
        compiler_params=pltpu.CompilerParams(
            collective_id=0, has_side_effects=True, vmem_limit_bytes=60 << 20
        ),
        cost_estimate=pl.CostEstimate(flops=0, bytes_accessed=300_000_000, transcendentals=0),
    )(
        states, norm_gain, final_gain, w_gate, w_up, w_down_t, w_proj, cent_ids >> 7, lens,
        cent_ids & 127, codes, spread, tables, which, table,
    )


def coords(shape):
    me = lax.axis_index("shard")
    return me // (2 * shape), (me // 2) % shape, me % 2, lax.axis_index("grp")


def ranks(hits):
    count = hits.shape[1]
    before = lax.broadcasted_iota(jnp.int32, (count, count), 0) < lax.broadcasted_iota(
        jnp.int32, (count, count), 1
    )
    return jnp.dot(
        hits.astype(jnp.bfloat16), before.astype(jnp.bfloat16), preferred_element_type=jnp.float32
    ).astype(jnp.int32)


def slots(hits, caps):
    nth = lax.broadcasted_iota(jnp.int32, (1, caps, 1), 1)
    return hits[:, None, :] & (ranks(hits)[:, None, :] == nth)


def local(
    query_states,
    norm_gain,
    final_gain,
    w_gate,
    w_up,
    w_down_t,
    w_proj,
    centroids,
    bucket_values,
    centroid_ids,
    residual_codes,
    passage_lens,
    negative_ids,
):
    q_dev, q_len, width = query_states.shape
    dim = w_proj.shape[1]
    shards = lax.axis_size("shard")
    side = math.isqrt(shards // 2)
    cands = negative_ids.shape[1]
    tok_rows = q_dev * q_len
    local_pass = centroid_ids.shape[0]
    caps = 2 * q_dev * cands // shards
    me = lax.axis_index("shard")

    flat_ids = negative_ids.reshape(1, -1)
    owner = lax.broadcasted_iota(jnp.int32, (shards, 1), 0)
    places = lax.broadcasted_iota(jnp.int32, (1, 1, q_dev * cands), 2)
    sent = slots(flat_ids // local_pass == owner, caps)
    place = jnp.sum(jnp.where(sent, places, 0), axis=2)
    asked = jnp.sum(jnp.where(sent, (flat_ids % local_pass)[:, None, :], 0), axis=2)
    tables = jnp.concatenate(
        [asked, place // cands, jnp.zeros((shards, 128 - 2 * caps), jnp.int32)], axis=1
    ).reshape(shards, 1, 128)
    lens = lax.dynamic_slice(passage_lens, (me * local_pass,), (local_pass,))
    states = query_states.reshape(tok_rows, width)
    filled = jnp.any(sent, axis=2)[:, :, None]
    query = lax.broadcasted_iota(jnp.int32, (1, 1, 128), 2)
    mine = filled & ((place // cands)[:, :, None] == query)
    first = mine & ((place % cands)[:, :, None] == 0)
    which = mine.astype(jnp.int32) + first.astype(jnp.int32)
    which = jnp.pad(which, ((0, 0), (0, 8 - caps), (0, 0))).reshape(shards * 8, 128)
    losses, grad_gate, grad_up, grad_down, grad_proj = step_call(
        states, norm_gain.reshape(1, -1), final_gain.reshape(1, -1), w_gate.T, w_up.T, w_down_t.T,
        w_proj, centroid_ids, lens, residual_codes, bucket_values, tables, which, centroids, side,
        caps, q_len,
    )
    return (losses[0, :q_dev], grad_gate, grad_up, grad_down, grad_proj)


def solution(mesh):
    placed = (
        P(("shard", "grp"), None, None),
        P(),
        P(),
        P(None, "grp"),
        P(None, "grp"),
        P(None, "grp"),
        P(),
        P("grp", None),
        P(None, "grp"),
        P("shard", None),
        P("shard", "grp", None),
        P(),
        P(("shard", "grp"), None),
    )
    return jax.shard_map(
        local,
        mesh=mesh,
        in_specs=placed,
        out_specs=(
            P(("shard", "grp")),
            P("shard", "grp"),
            P("shard", "grp"),
            P("shard", "grp"),
            P(("shard", "grp"), None),
        ),
        check_vma=False,
    )
```

```python
import functools
import math

import jax
import jax.numpy as jnp
from jax import lax
from jax.experimental import pallas as pl
from jax.experimental.pallas import tpu as pltpu
from jax.sharding import PartitionSpec as P

MESH = pl.DeviceIdType.MESH


def layer_norm(rows, gain):
    centre = rows - jnp.mean(rows, axis=-1, keepdims=True)
    spread = jnp.mean(centre * centre, axis=-1, keepdims=True)
    return centre * lax.rsqrt(spread + 1e-05) * gain


def rebuild_passage(p, blk_ref, lane_ref, codes_ref, bucket_ref, tab):
    dims, toks = tab.shape[0], lane_ref.shape[1]
    lane = lax.broadcasted_iota(jnp.int32, (dims, toks), 1)
    shift = 2 * lax.broadcasted_iota(jnp.int32, (8, toks), 0)
    spot = jnp.broadcast_to(lane_ref[pl.ds(p, 1), :], (dims, toks))
    base = jnp.zeros((dims, toks), jnp.float32)
    for j in range(toks):
        block = tab[:, pl.ds(blk_ref[p, j] * 128, 128)].astype(jnp.float32)
        base = jnp.where(lane == j, jnp.take_along_axis(block, spot, axis=1), base)
    words = codes_ref[p]
    fields = jnp.concatenate(
        [
            jnp.bitwise_and(
                jnp.right_shift(jnp.broadcast_to(words[w : w + 1], (8, toks)), shift), 3
            )
            for w in range(dims // 8)
        ],
        axis=0,
    )
    resid = jnp.where(
        fields < 2,
        jnp.where(fields == 0, bucket_ref[0], bucket_ref[1]),
        jnp.where(fields == 2, bucket_ref[2], bucket_ref[3]),
    )
    return (base + resid).astype(jnp.bfloat16)


def dot_t(left, right):
    return lax.dot_general(
        left, right, (((1,), (1,)), ((), ())), preferred_element_type=jnp.float32
    )


def pair(docs, queries, count):
    q_len, dim = queries.shape
    toks = docs.shape[1]
    spots = lax.broadcasted_iota(jnp.int32, (q_len, toks), 1)
    values = docs.astype(jnp.float32)
    scale = lax.rsqrt(jnp.mean(values * values, axis=0, keepdims=True) + 1e-06) / math.sqrt(dim)
    sims = jnp.dot(queries, docs, preferred_element_type=jnp.float32)
    raised = jnp.where(spots < count, jnp.exp(64.0 * (sims * scale)), 0.0)
    total = jnp.sum(raised, axis=1, keepdims=True)
    score = jnp.sum(jnp.log(total), axis=0, keepdims=True) / 64.0
    pull = dot_t((raised * (scale / total)).astype(jnp.bfloat16), docs)
    return pull.astype(jnp.bfloat16), score


def step_kernel(
    side, groups, chunks,
    states_ref, norm_gain_ref, final_gain_ref, gate_w, up_w, down_w, proj_w,
    blk_ref, lens_ref, lane_ref, codes_ref, bucket_ref, tables_ref, which_ref, tab_hbm,
    loss_ref, gate_out, up_out, down_out, proj_out,
    tab, docs, rows_ref, slope_ref, gelu_ref, hidden_ref, part, part_own, part_tmp, part_in, out_ref,
    final_t, proj_ref, asks, asks_smem, queries, pull_out, score_out, pull_ref, score_ref,
    weights, douts, rows_t, douts_t, dgate, dup, first, twin, held,
    tmp_one, in_one, mids, tmp_two, in_two,
    proj_term, twin_proj, held_proj, land_proj, rows_sum, land_grp,
    tab_sem, asks_sem, rows_send, rows_recv, dout_send, dout_recv,
    grp_send, grp_recv, docs_send, docs_recv, ring_send, ring_recv,
    asks_send, asks_recv, pull_send, pull_recv, score_send, score_recv,
    twin_send, twin_recv, chip_send, chip_recv,
):
    z, x, core, grp = coords(side)
    me = (z * side + x) * 2 + core
    shards = 2 * side * side
    passages, toks = lane_ref.shape
    span = passages // chunks
    tok_rows = states_ref.shape[0]
    caps, q_len, dim = pull_ref.shape[1:]

    pieces = tab_sem.shape[0]
    width = tab.shape[1] // pieces
    table_copies = [
        pltpu.make_async_copy(
            tab_hbm.at[:, pl.ds(i * width, width)], tab.at[:, pl.ds(i * width, width)], tab_sem.at[i]
        )
        for i in range(pieces)
    ]
    for copy in table_copies:
        copy.start()

    def to(step):
        dz, dx, dc = step // (2 * side), (step // 2) % side, step % 2
        return (((z + dz) % side) * side + (x + dx) % side) * 2 + (core + dc) % 2

    def source(step):
        dz, dx, dc = step // (2 * side), (step // 2) % side, step % 2
        return (
            ((z + side - dz) % side) * side + (x + side - dx) % side
        ) * 2 + (core + 2 - dc) % 2

    barrier = pltpu.get_barrier_semaphore()

    def greet(step, carry):
        pl.semaphore_signal(barrier, inc=1, device_id=(to(step), grp), device_id_type=MESH)
        return carry

    lax.fori_loop(1, shards, greet, 0)
    for step in range(1, groups):
        pl.semaphore_signal(
            barrier, inc=1, device_id=(me, (grp + step) % groups), device_id_type=MESH
        )
    rows_ref[grp] = layer_norm(states_ref[...].astype(jnp.float32), norm_gain_ref[...]).astype(
        jnp.bfloat16
    )
    pl.semaphore_wait(barrier, shards + groups - 2)

    def along_grp(step, src, dst, send_sem, recv_sem):
        return pltpu.make_async_remote_copy(
            src_ref=src, dst_ref=dst, send_sem=send_sem, recv_sem=recv_sem,
            device_id=(me, (grp + step) % groups), device_id_type=MESH,
        )

    left, right, across = (grp + groups - 1) % groups, (grp + 1) % groups, (grp + 2) % groups

    def spread_grp(view, send_sem, recv_sem):
        def copy(j, incoming):
            slot = ((left, right, across, across) if incoming else (grp, grp, left, right))[j]
            place = view(slot, None if j < 2 else j - 2)
            return pltpu.make_async_remote_copy(
                src_ref=place, dst_ref=place, send_sem=send_sem(j), recv_sem=recv_sem(j),
                device_id=(me, left if j % 2 else right), device_id_type=MESH,
            )

        return copy

    def rows_view(ref):
        half = tok_rows // 2
        return lambda slot, part: (
            ref.at[slot] if part is None else ref.at[slot, pl.ds(part * half, half)]
        )

    rows_copy = spread_grp(
        rows_view(rows_ref), lambda j: rows_send.at[j], lambda j: rows_recv.at[j]
    )
    dout_copy = spread_grp(rows_view(douts), lambda j: dout_send.at[j], lambda j: dout_recv.at[j])

    def docs_copies(c):
        half = span // 2
        return spread_grp(
            lambda slot, part: (
                docs.at[slot, pl.ds(c * span, span)]
                if part is None
                else docs.at[slot, pl.ds(c * span + part * half, half)]
            ),
            lambda j: docs_send.at[c, j],
            lambda j: docs_recv.at[c, j],
        )

    def docs_own(c):
        copy = docs_copies(c)
        copy(0, False).start()
        copy(1, False).start()

    def docs_forward(c):
        copy = docs_copies(c)
        for j in range(2):
            copy(j, True).wait_recv()
            copy(j + 2, False).start()

    def sum_ring(n, lower, upper, view, tmp, into):
        def copy(j):
            src = (view(2, 0), view(2, 1), view(3, None), view(1, None))[j]
            return pltpu.make_async_remote_copy(
                src_ref=src, dst_ref=(tmp.at[j] if j < 2 else into.at[j - 2]),
                send_sem=ring_send.at[n, j], recv_sem=ring_recv.at[n, j],
                device_id=upper if j % 2 else lower, device_id_type=MESH,
            )

        def start():
            copy(0).start()
            copy(1).start()

        def middle():
            for j in range(2):
                copy(j).wait_recv()
                place = view(1 if j else 3, j)
                place[...] = (
                    place[...].astype(jnp.float32) + tmp[j].astype(jnp.float32)
                ).astype(jnp.bfloat16)
                copy(j + 2).start()

        def end():
            copy(2).wait_recv()
            copy(3).wait_recv()
            return into[0].astype(jnp.float32) + into[1].astype(jnp.float32)

        def sent():
            for j in range(4):
                copy(j).wait_send()

        return start, middle, end, sent

    def part_view(k, half):
        slot = (grp + k) % groups
        rows = tok_rows // 2
        return part.at[slot] if half is None else part.at[slot, pl.ds(half * rows, rows)]

    part_start, part_middle, part_end, part_sent = sum_ring(
        0, (me, left), (me, right), part_view, part_tmp, part_in
    )

    def along_shard(step, src, dst, send_sems, recv_sems):
        return pltpu.make_async_remote_copy(
            src_ref=src, dst_ref=dst, send_sem=send_sems.at[step], recv_sem=recv_sems.at[step],
            device_id=(to(step), grp), device_id_type=MESH,
        )

    def asks_copy(step, slot):
        return along_shard(step, tables_ref.at[to(step)], asks.at[slot], asks_send, asks_recv)

    chips = side * side
    chip = me // 2

    def chip_to(step):
        return ((z + step // side) % side) * side + (x + step % side) % side

    def chip_from(step):
        return ((z + side - step // side) % side) * side + (x + side - step % side) % side

    def query_copy(step, slot):
        return pltpu.make_async_remote_copy(
            src_ref=queries.at[chip, core], dst_ref=queries.at[slot, core],
            send_sem=chip_send.at[1, step - 1], recv_sem=chip_recv.at[1, step - 1],
            device_id=(chip_to(step) * 2 + core, grp), device_id_type=MESH,
        )

    def swap(src, dst, i):
        return pltpu.make_async_remote_copy(
            src_ref=src, dst_ref=dst, send_sem=twin_send.at[i], recv_sem=twin_recv.at[i],
            device_id=(chip * 2 + 1 - core, grp), device_id_type=MESH,
        )

    def query_swap(of):
        return swap(queries.at[:, of], queries.at[:, of], side + 1)

    def back(step, src, dst, send_sems, recv_sems):
        return pltpu.make_async_remote_copy(
            src_ref=src, dst_ref=dst, send_sem=send_sems.at[step], recv_sem=recv_sems.at[step],
            device_id=(source(step), grp), device_id_type=MESH,
        )

    def pull_copy(step, slot):
        return back(step, pull_out.at[source(step)], pull_ref.at[slot], pull_send, pull_recv)

    def score_copy(step, slot):
        return back(step, score_out.at[source(step)], score_ref.at[slot], score_send, score_recv)

    rows_copy(0, False).start()
    rows_copy(1, False).start()

    def ask(step, carry):
        asks_copy(step, me).start()
        return carry

    lax.fori_loop(1, shards, ask, 0)
    asks[me] = tables_ref[me]
    for j in range(2):
        rows_copy(j, True).wait_recv()
        rows_copy(j + 2, False).start()
    for copy in table_copies:
        copy.wait()

    def feed_forward():
        rows_copy(2, True).wait_recv()
        rows_copy(3, True).wait_recv()

        def block(r, carry):
            normed = rows_ref[r]
            gate = dot_t(normed, gate_w[...])
            up = dot_t(normed, up_w[...])
            cdf = 0.5 * (1.0 + lax.erf(gate * (1.0 / math.sqrt(2.0))))
            gelu = gate * cdf
            bell = jnp.exp(-0.5 * gate * gate) * (1.0 / math.sqrt(2.0 * math.pi))
            slope_ref[r] = ((cdf + gate * bell) * up).astype(jnp.bfloat16)
            gelu_ref[r] = gelu.astype(jnp.bfloat16)
            hidden = (gelu * up).astype(jnp.bfloat16)
            hidden_ref[r] = hidden
            down = jnp.dot(hidden, down_w[...], preferred_element_type=jnp.float32)
            part[r] = down.astype(jnp.bfloat16)

            @pl.when(r == grp)
            def _():
                part_own[...] = down

            return carry

        lax.fori_loop(0, groups, block, 0)
        part_start()

    def make_queries():
        out = states_ref[...].astype(jnp.float32) + part_own[...] + part_end()
        out_ref[...] = out
        final = layer_norm(out, final_gain_ref[...]).astype(jnp.bfloat16)
        final_t[...] = final.T
        proj = jnp.dot(final, proj_w[...], preferred_element_type=jnp.float32)
        proj_ref[...] = proj
        scale = lax.rsqrt(jnp.mean(proj * proj, axis=-1, keepdims=True) + 1e-06) / math.sqrt(dim)
        queries[chip, core] = (proj * scale).astype(jnp.bfloat16).reshape(tok_rows // q_len, q_len, dim)

        def tell(step, carry):
            query_copy(step, chip).start()
            return carry

        lax.fori_loop(1, chips, tell, 0)

    def chunk_of(c, carry):
        def passage(i, carry):
            p = c * span + i
            docs[grp, p] = rebuild_passage(p, blk_ref, lane_ref, codes_ref, bucket_ref, tab)
            return carry

        lax.fori_loop(0, span, passage, 0)
        docs_own(c)
        pl.when(c > 0)(lambda: docs_forward(c - 1))
        pl.when(c == 0)(feed_forward)
        pl.when(c == 1)(part_middle)
        pl.when(c == 3)(make_queries)
        return carry

    lax.fori_loop(0, chunks, chunk_of, 0)

    docs_forward(chunks - 1)

    def queries_in(step, carry):
        query_copy(step, chip_from(step)).wait_recv()
        return carry

    lax.fori_loop(1, chips, queries_in, 0)
    query_swap(core).start()

    def gather_in(step, carry):
        asks_copy(step, source(step)).wait_recv()
        return carry

    lax.fori_loop(1, shards, gather_in, 0)
    to_smem = pltpu.make_async_copy(asks, asks_smem, asks_sem)
    to_smem.start()
    to_smem.wait()

    query_swap(1 - core).wait_recv()

    def docs_in(c, carry):
        docs_copies(c)(2, True).wait_recv()
        docs_copies(c)(3, True).wait_recv()
        return carry

    lax.fori_loop(0, chunks, docs_in, 0)

    def serve(step, carry):
        d = source(step)
        rows = []
        for k in range(caps):
            p = asks_smem[d, 0, k]
            raw = jnp.concatenate([docs[g, p] for g in range(groups)], axis=0)
            pull, score = pair(raw, queries[d // 2, d % 2, asks_smem[d, 0, caps + k]], lens_ref[p])
            pull_out[d, k] = pull
            rows.append(jnp.broadcast_to(score, (1, dim)))
        score_out[d] = jnp.concatenate(rows + [jnp.zeros((8 - caps, dim), jnp.float32)], axis=0)

        @pl.when(step > 0)
        def _():
            pull_copy(step, me).start()
            score_copy(step, me).start()

        @pl.when(step == 0)
        def _():
            pull_ref[me] = pull_out[me]
            score_ref[me] = score_out[me]

        return carry

    lax.fori_loop(0, shards, serve, 0)

    for r in range(groups):
        turned = rows_ref[r].T.reshape(side * side, 2, rows_t.shape[2], tok_rows)
        rows_t[:, :, :, r * tok_rows : (r + 1) * tok_rows] = turned

    def finish(step, carry):
        pull_copy(step, to(step)).wait_recv()
        score_copy(step, to(step)).wait_recv()
        return carry

    lax.fori_loop(1, shards, finish, 0)

    which = which_ref[...]
    scores = 10.0 * score_ref[...].reshape(which.shape)
    top = jnp.max(jnp.where(which > 0, scores, -1e30), axis=0, keepdims=True)
    raised = jnp.where(which > 0, jnp.exp(scores - top), 0.0)
    total = jnp.sum(raised, axis=0, keepdims=True)
    chosen = jnp.sum(jnp.where(which == 2, scores, 0.0), axis=0, keepdims=True)
    loss_ref[...] = jnp.broadcast_to(top + jnp.log(total) - chosen, loss_ref.shape)
    spread = 10.0 * (raised / total - jnp.where(which == 2, 1.0, 0.0))
    q_dev = tok_rows // q_len
    for q in range(q_dev):
        weights[q] = jnp.broadcast_to(spread[:, q : q + 1], spread.shape).reshape(
            weights.shape[1:]
        )

    def gather_pull(s, sums):
        sums = list(sums)
        for k in range(caps):
            term = pull_ref[s, k].astype(jnp.float32)
            for q in range(q_dev):
                sums[q] = sums[q] + weights[q, s, k : k + 1, :] * term
        return tuple(sums)

    zero = jnp.zeros((q_len, dim), jnp.float32)
    sums = lax.fori_loop(0, shards, gather_pull, (zero,) * q_dev)
    dqueries = jnp.concatenate(sums, axis=0).astype(jnp.bfloat16).astype(jnp.float32)
    proj = proj_ref[...]
    length = lax.rsqrt(jnp.mean(proj * proj, axis=-1, keepdims=True) + 1e-06)
    along = jnp.mean(dqueries * proj, axis=-1, keepdims=True)
    dproj = (
        (length / math.sqrt(dim)) * (dqueries - proj * (length * length * along))
    ).astype(jnp.bfloat16)

    dfinal = dot_t(dproj, proj_w[...]) * final_gain_ref[...]
    out = out_ref[...]
    centre = out - jnp.mean(out, axis=-1, keepdims=True)
    inverse = lax.rsqrt(jnp.mean(centre * centre, axis=-1, keepdims=True) + 1e-05)
    unit = centre * inverse
    dout = inverse * (
        dfinal
        - jnp.mean(dfinal, axis=-1, keepdims=True)
        - unit * jnp.mean(dfinal * unit, axis=-1, keepdims=True)
    )
    douts[grp] = dout.astype(jnp.bfloat16)

    dout_copy(0, False).start()
    dout_copy(1, False).start()

    block = rows_t.shape[2]

    def chip_copy(step):
        return pltpu.make_async_remote_copy(
            src_ref=held_proj.at[chip_to(step)], dst_ref=land_proj.at[step - 1],
            send_sem=chip_send.at[0, step - 1], recv_sem=chip_recv.at[0, step - 1],
            device_id=(chip_to(step) * 2 + core, grp), device_id_type=MESH,
        )

    proj_term[...] = jnp.dot(
        final_t[...], dproj, preferred_element_type=jnp.float32
    ).reshape(proj_term.shape)
    proj_swap = swap(proj_term.at[:, 1 - core], twin_proj, side)
    proj_swap.start()

    def spread_back(i, carry):
        @pl.when(i == 1)
        def _():
            for j in range(2):
                dout_copy(j, True).wait_recv()
                dout_copy(j + 2, False).start()

        @pl.when(i == 3)
        def _():
            dout_copy(2, True).wait_recv()
            dout_copy(3, True).wait_recv()

        r = (grp + i + i // 2 - 2 * (i // 3)) % groups
        dhid = dot_t(douts[r], down_w[...])
        dgate[r] = (dhid * slope_ref[r].astype(jnp.float32)).astype(jnp.bfloat16)
        dup[r] = (dhid * gelu_ref[r].astype(jnp.float32)).astype(jnp.bfloat16)
        return carry

    lax.fori_loop(0, groups, spread_back, 0)
    for r in range(groups):
        turned = douts[r].T.reshape(chips, 2, block, tok_rows)
        douts_t[:, :, :, r * tok_rows : (r + 1) * tok_rows] = turned

    proj_swap.wait_recv()

    def add_proj(c, carry):
        held_proj[c] = proj_term[c, core] + twin_proj[c]
        return carry

    lax.fori_loop(0, chips, add_proj, 0)

    def send_proj(step, carry):
        chip_copy(step).start()
        return carry

    lax.fori_loop(1, chips, send_proj, 0)

    tokens = groups * tok_rows

    main = gate_out.shape[1] // 128 * 128
    rest = gate_out.shape[1] - main

    def terms(row, half):
        found = []
        for lhs, rhs in ((rows_t, dgate), (rows_t, dup), (douts_t, hidden_ref)):
            found.append(
                jnp.dot(
                    lhs[pl.ds(row * side, side), half].reshape(side * block, tokens),
                    rhs[...].reshape(tokens, main + rest),
                    preferred_element_type=jnp.float32,
                )
            )
        fill = jnp.zeros((side * block, held.shape[3] - 3 * (main + rest)), jnp.float32)
        return jnp.concatenate(
            [t[:, :main] for t in found] + [t[:, main:] for t in found] + [fill], axis=1
        ).reshape(side, block, held.shape[3])

    def row_of(i):
        return (z + 2 + i) % side

    def swap_copy(i):
        return swap(first.at[row_of(i)], twin.at[row_of(i)], i)

    def give(i, carry):
        first[row_of(i)] = terms(row_of(i), 1 - core).astype(jnp.bfloat16)
        swap_copy(i).start()
        return carry

    lax.fori_loop(0, side, give, 0)

    cols = held.shape[3] // 2
    few = side // 2
    x_low = ((z * side + (x + side - 1) % side) * 2 + core, grp)
    x_high = ((z * side + (x + 1) % side) * 2 + core, grp)
    z_low = ((((z + side - 1) % side) * side + x) * 2 + core, grp)
    z_high = ((((z + 1) % side) * side + x) * 2 + core, grp)

    def view_x(k, half):
        rows = pl.ds(0, side) if half is None else pl.ds(half * few, few)
        return held.at[rows, (x + k) % side, :, pl.ds(0, cols)]

    def view_z(k, half):
        rows = pl.ds(0, side) if half is None else pl.ds(half * few, few)
        return held.at[(z + k) % side, rows, :, pl.ds(cols, cols)]

    def view_mid(n, place):
        def view(k, half):
            spot = (place + k) % side
            part = block // 2
            return mids.at[n, spot] if half is None else mids.at[n, spot, pl.ds(half * part, part)]

        return view

    ring_x = sum_ring(1, x_low, x_high, view_x, tmp_one.at[0], in_one.at[0])
    ring_z = sum_ring(2, z_low, z_high, view_z, tmp_one.at[1], in_one.at[1])
    then_z = sum_ring(3, z_low, z_high, view_mid(0, z), tmp_two.at[0], in_two.at[0])
    then_x = sum_ring(4, x_low, x_high, view_mid(1, x), tmp_two.at[1], in_two.at[1])

    def keep(i, carry):
        swap_copy(i).wait_recv()
        held[row_of(i)] = (
            terms(row_of(i), core) + twin[row_of(i)].astype(jnp.float32)
        ).astype(jnp.bfloat16)
        pl.when(i == 0)(ring_z[0])
        return carry

    lax.fori_loop(0, side, keep, 0)
    ring_x[0]()
    ring_z[1]()
    ring_x[1]()

    def proj_in(step, total):
        chip_copy(step).wait_recv()
        return total + land_proj[step - 1]

    rows_sum[...] = lax.fori_loop(1, chips, proj_in, held_proj[chip]).reshape(rows_sum.shape)

    def sum_copy(step):
        return along_grp(
            step, rows_sum.at[(grp + step) % groups], land_grp.at[step - 1],
            grp_send.at[step], grp_recv.at[step],
        )

    for step in range(1, groups):
        sum_copy(step).start()
    mine = rows_sum[grp]
    for step in range(1, groups):
        sum_copy(step).wait_recv()
        mine = mine + land_grp[step - 1]
    proj_out[...] = mine

    mids[1] = (view_z(0, None)[...].astype(jnp.float32) + ring_z[2]()).astype(jnp.bfloat16)
    then_x[0]()
    mids[0] = (view_x(0, None)[...].astype(jnp.float32) + ring_x[2]()).astype(jnp.bfloat16)
    then_z[0]()
    then_x[1]()
    then_z[1]()
    whole = jnp.concatenate(
        [
            mids[0, z].astype(jnp.float32) + then_z[2](),
            mids[1, x].astype(jnp.float32) + then_x[2](),
        ],
        axis=1,
    )
    for n, ref in enumerate((gate_out, up_out, down_out)):
        ref[:, :main] = whole[:, n * main : (n + 1) * main]
        ref[:, main:] = whole[:, 3 * main + n * rest : 3 * main + (n + 1) * rest]

    def sent(step, carry):
        asks_copy(step, me).wait_send()
        pull_copy(step, me).wait_send()
        score_copy(step, me).wait_send()
        return carry

    lax.fori_loop(1, shards, sent, 0)
    for step in range(1, groups):
        sum_copy(step).wait_send()
    for j in range(4):
        rows_copy(j, False).wait_send()
        dout_copy(j, False).wait_send()
    for ring in (ring_x, ring_z, then_x, then_z):
        ring[3]()
    part_sent()
    query_swap(core).wait_send()

    def docs_out(c, carry):
        for j in range(4):
            docs_copies(c)(j, False).wait_send()
        return carry

    lax.fori_loop(0, chunks, docs_out, 0)
    proj_swap.wait_send()

    def swapped(i, carry):
        swap_copy(i).wait_send()
        return carry

    lax.fori_loop(0, side, swapped, 0)

    def chips_out(step, carry):
        chip_copy(step).wait_send()
        query_copy(step, chip).wait_send()
        return carry

    lax.fori_loop(1, chips, chips_out, 0)


def step_call(
    states, norm_gain, final_gain, w_gate, w_up, w_down_t, w_proj, cent_ids, lens, codes, bucket,
    tables, which, table, side, caps, q_len,
):
    groups = lax.axis_size("grp")
    shards = 2 * side * side
    chips = side * side
    tok_rows, width = states.shape
    part = w_gate.shape[0]
    dim = w_proj.shape[1]
    passages, toks = cent_ids.shape
    dims, count = table.shape
    chunks = 8
    block = width // shards
    tokens = groups * tok_rows
    spread = jnp.broadcast_to(bucket[:, :, None], (4, dims, toks))
    vmem = pl.BlockSpec(memory_space=pltpu.VMEM)
    smem = pl.BlockSpec(memory_space=pltpu.SMEM)
    bf16, f32 = jnp.bfloat16, jnp.float32
    dma = pltpu.SemaphoreType.DMA
    wide = (side, side, block, -(-3 * part // 256) * 256)
    cols = wide[3] // 2
    return pl.pallas_call(
        functools.partial(step_kernel, side, groups, chunks),
        out_shape=(jax.ShapeDtypeStruct((8, 128), f32),)
        + (jax.ShapeDtypeStruct((block, part), f32),) * 3
        + (jax.ShapeDtypeStruct((block // groups, dim), f32),),
        in_specs=[vmem] * 7 + [smem] * 2 + [vmem] * 5 + [pl.BlockSpec(memory_space=pl.ANY)],
        out_specs=(vmem,) * 5,
        scratch_shapes=[
            pltpu.VMEM((dims, count), bf16),
            pltpu.VMEM((groups, passages, dims, toks), bf16),
            pltpu.VMEM((groups, tok_rows, width), bf16),
            pltpu.VMEM((groups, tok_rows, part), bf16),
            pltpu.VMEM((groups, tok_rows, part), bf16),
            pltpu.VMEM((groups, tok_rows, part), bf16),
            pltpu.VMEM((groups, tok_rows, width), bf16),
            pltpu.VMEM((tok_rows, width), f32),
            pltpu.VMEM((2, tok_rows // 2, width), bf16),
            pltpu.VMEM((2, tok_rows, width), bf16),
            pltpu.VMEM((tok_rows, width), f32),
            pltpu.VMEM((width, tok_rows), bf16),
            pltpu.VMEM((tok_rows, dim), f32),
            pltpu.VMEM((shards, 1, 128), jnp.int32),
            pltpu.SMEM((shards, 1, 128), jnp.int32),
            pltpu.VMEM((chips, 2, tok_rows // q_len, q_len, dim), bf16),
            pltpu.VMEM((shards, caps, q_len, dim), bf16),
            pltpu.VMEM((shards, 8, dim), f32),
            pltpu.VMEM((shards, caps, q_len, dim), bf16),
            pltpu.VMEM((shards, 8, dim), f32),
            pltpu.VMEM((tok_rows // q_len, shards, 8, dim), f32),
            pltpu.VMEM((groups, tok_rows, width), bf16),
            pltpu.VMEM((chips, 2, block, tokens), bf16),
            pltpu.VMEM((chips, 2, block, tokens), bf16),
            pltpu.VMEM((groups, tok_rows, part), bf16),
            pltpu.VMEM((groups, tok_rows, part), bf16),
            pltpu.VMEM(wide, bf16),
            pltpu.VMEM(wide, bf16),
            pltpu.VMEM(wide, bf16),
            pltpu.VMEM((2, 2, side // 2, block, cols), bf16),
            pltpu.VMEM((2, 2, side, block, cols), bf16),
            pltpu.VMEM((2, side, block, cols), bf16),
            pltpu.VMEM((2, 2, block // 2, cols), bf16),
            pltpu.VMEM((2, 2, block, cols), bf16),
            pltpu.VMEM((chips, 2, block, dim), f32),
            pltpu.VMEM((chips, block, dim), f32),
            pltpu.VMEM((chips, block, dim), f32),
            pltpu.VMEM((chips - 1, block, dim), f32),
            pltpu.VMEM((groups, block // groups, dim), f32),
            pltpu.VMEM((groups - 1, block // groups, dim), f32),
            dma((8,)),
            dma,
        ]
        + [dma((groups,))] * 6
        + [dma((chunks, groups))] * 2
        + [dma((5, groups))] * 2
        + [dma((shards,))] * 6
        + [dma((side + 2,))] * 2
        + [dma((2, chips - 1))] * 2,
        compiler_params=pltpu.CompilerParams(
            collective_id=0, has_side_effects=True, vmem_limit_bytes=60 << 20
        ),
        cost_estimate=pl.CostEstimate(flops=0, bytes_accessed=300_000_000, transcendentals=0),
    )(
        states, norm_gain, final_gain, w_gate, w_up, w_down_t, w_proj, cent_ids >> 7, lens,
        cent_ids & 127, codes, spread, tables, which, table,
    )


def coords(shape):
    me = lax.axis_index("shard")
    return me // (2 * shape), (me // 2) % shape, me % 2, lax.axis_index("grp")


def ranks(hits):
    count = hits.shape[1]
    before = lax.broadcasted_iota(jnp.int32, (count, count), 0) < lax.broadcasted_iota(
        jnp.int32, (count, count), 1
    )
    return jnp.dot(
        hits.astype(jnp.bfloat16), before.astype(jnp.bfloat16), preferred_element_type=jnp.float32
    ).astype(jnp.int32)


def slots(hits, caps):
    nth = lax.broadcasted_iota(jnp.int32, (1, caps, 1), 1)
    return hits[:, None, :] & (ranks(hits)[:, None, :] == nth)


def local(
    query_states,
    norm_gain,
    final_gain,
    w_gate,
    w_up,
    w_down_t,
    w_proj,
    centroids,
    bucket_values,
    centroid_ids,
    residual_codes,
    passage_lens,
    negative_ids,
):
    q_dev, q_len, width = query_states.shape
    dim = w_proj.shape[1]
    shards = lax.axis_size("shard")
    side = math.isqrt(shards // 2)
    cands = negative_ids.shape[1]
    tok_rows = q_dev * q_len
    local_pass = centroid_ids.shape[0]
    caps = 2 * q_dev * cands // shards
    me = lax.axis_index("shard")

    flat_ids = negative_ids.reshape(1, -1)
    owner = lax.broadcasted_iota(jnp.int32, (shards, 1), 0)
    places = lax.broadcasted_iota(jnp.int32, (1, 1, q_dev * cands), 2)
    sent = slots(flat_ids // local_pass == owner, caps)
    place = jnp.sum(jnp.where(sent, places, 0), axis=2)
    asked = jnp.sum(jnp.where(sent, (flat_ids % local_pass)[:, None, :], 0), axis=2)
    tables = jnp.concatenate(
        [asked, place // cands, jnp.zeros((shards, 128 - 2 * caps), jnp.int32)], axis=1
    ).reshape(shards, 1, 128)
    lens = lax.dynamic_slice(passage_lens, (me * local_pass,), (local_pass,))
    states = query_states.reshape(tok_rows, width)
    filled = jnp.any(sent, axis=2)[:, :, None]
    query = lax.broadcasted_iota(jnp.int32, (1, 1, 128), 2)
    mine = filled & ((place // cands)[:, :, None] == query)
    first = mine & ((place % cands)[:, :, None] == 0)
    which = mine.astype(jnp.int32) + first.astype(jnp.int32)
    which = jnp.pad(which, ((0, 0), (0, 8 - caps), (0, 0))).reshape(shards * 8, 128)
    losses, grad_gate, grad_up, grad_down, grad_proj = step_call(
        states, norm_gain.reshape(1, -1), final_gain.reshape(1, -1), w_gate.T, w_up.T, w_down_t.T,
        w_proj, centroid_ids, lens, residual_codes, bucket_values, tables, which, centroids, side,
        caps, q_len,
    )
    return (losses[0, :q_dev], grad_gate, grad_up, grad_down, grad_proj)


def solution(mesh):
    placed = (
        P(("shard", "grp"), None, None),
        P(),
        P(),
        P(None, "grp"),
        P(None, "grp"),
        P(None, "grp"),
        P(),
        P("grp", None),
        P(None, "grp"),
        P("shard", None),
        P("shard", "grp", None),
        P(),
        P(("shard", "grp"), None),
    )
    return jax.shard_map(
        local,
        mesh=mesh,
        in_specs=placed,
        out_specs=(
            P(("shard", "grp")),
            P("shard", "grp"),
            P("shard", "grp"),
            P("shard", "grp"),
            P(("shard", "grp"), None),
        ),
        check_vma=False,
    )
```

```python
import functools
import math

import jax
import jax.numpy as jnp
from jax import lax
from jax.experimental import pallas as pl
from jax.experimental.pallas import tpu as pltpu
from jax.sharding import PartitionSpec as P

MESH = pl.DeviceIdType.MESH


def layer_norm(rows, gain):
    centre = rows - jnp.mean(rows, axis=-1, keepdims=True)
    spread = jnp.mean(centre * centre, axis=-1, keepdims=True)
    return centre * lax.rsqrt(spread + 1e-05) * gain


def rebuild_passage(p, blk_ref, lane_ref, codes_ref, bucket_ref, tab):
    dims, toks = tab.shape[0], lane_ref.shape[1]
    lane = lax.broadcasted_iota(jnp.int32, (dims, toks), 1)
    shift = 2 * lax.broadcasted_iota(jnp.int32, (8, toks), 0)
    spot = jnp.broadcast_to(lane_ref[pl.ds(p, 1), :], (dims, toks))
    base = jnp.zeros((dims, toks), jnp.float32)
    for j in range(toks):
        block = tab[:, pl.ds(blk_ref[p, j] * 128, 128)].astype(jnp.float32)
        near = jnp.take_along_axis(block, spot, axis=1, mode="promise_in_bounds")
        base = jnp.where(lane == j, near, base)
    words = codes_ref[p]
    fields = jnp.concatenate(
        [
            jnp.bitwise_and(
                jnp.right_shift(jnp.broadcast_to(words[w : w + 1], (8, toks)), shift), 3
            )
            for w in range(dims // 8)
        ],
        axis=0,
    )
    resid = jnp.where(
        fields < 2,
        jnp.where(fields == 0, bucket_ref[0], bucket_ref[1]),
        jnp.where(fields == 2, bucket_ref[2], bucket_ref[3]),
    )
    return (base + resid).astype(jnp.bfloat16)


def dot_t(left, right):
    return lax.dot_general(
        left, right, (((1,), (1,)), ((), ())), preferred_element_type=jnp.float32
    )


def pair(docs, queries, count):
    q_len, dim = queries.shape
    toks = docs.shape[1]
    spots = lax.broadcasted_iota(jnp.int32, (q_len, toks), 1)
    values = docs.astype(jnp.float32)
    scale = lax.rsqrt(jnp.mean(values * values, axis=0, keepdims=True) + 1e-06) / math.sqrt(dim)
    sims = jnp.dot(queries, docs, preferred_element_type=jnp.float32)
    raised = jnp.where(spots < count, jnp.exp(64.0 * (sims * scale)), 0.0)
    total = jnp.sum(raised, axis=1, keepdims=True)
    score = jnp.sum(jnp.log(total), axis=0, keepdims=True) / 64.0
    pull = dot_t((raised * (scale / total)).astype(jnp.bfloat16), docs)
    return pull.astype(jnp.bfloat16), score


def step_kernel(
    side, groups, chunks,
    states_ref, norm_gain_ref, final_gain_ref, gate_hbm, up_hbm, down_hbm, proj_w,
    blk_ref, lens_ref, lane_ref, codes_ref, bucket_ref, tables_ref, which_ref, tab_hbm,
    loss_ref, gate_out, up_out, down_out, proj_out,
    tab, gate_w, up_w, down_w, docs, rows_ref, slope_ref, gelu_ref, hidden_ref, part, part_own, part_tmp, part_in, out_ref,
    final_t, proj_ref, asks, asks_smem, queries, pull_out, score_out, pull_ref, score_ref,
    weights, douts, rows_t, douts_t, dgate, dup, first, twin, held,
    tmp_one, in_one, mids, tmp_two, in_two,
    proj_term, twin_proj, held_proj, land_proj, rows_sum, land_grp,
    tab_sem, weight_sem, asks_sem, rows_send, rows_recv, dout_send, dout_recv,
    grp_send, grp_recv, docs_send, docs_recv, ring_send, ring_recv,
    asks_send, asks_recv, pull_send, pull_recv, score_send, score_recv,
    twin_send, twin_recv, chip_send, chip_recv,
):
    z, x, core, grp = coords(side)
    me = (z * side + x) * 2 + core
    shards = 2 * side * side
    passages, toks = lane_ref.shape
    span = passages // chunks
    tok_rows = states_ref.shape[0]
    caps, q_len, dim = pull_ref.shape[1:]

    pieces = tab_sem.shape[0]
    width = tab.shape[1] // pieces
    table_copies = [
        pltpu.make_async_copy(
            tab_hbm.at[:, pl.ds(i * width, width)], tab.at[:, pl.ds(i * width, width)], tab_sem.at[i]
        )
        for i in range(pieces)
    ]
    weight_copies = [
        pltpu.make_async_copy(src, dst, weight_sem.at[n])
        for n, (src, dst) in enumerate(((gate_hbm, gate_w), (up_hbm, up_w), (down_hbm, down_w)))
    ]
    for copy in table_copies + weight_copies:
        copy.start()

    def to(step):
        dz, dx, dc = step // (2 * side), (step // 2) % side, step % 2
        return (((z + dz) % side) * side + (x + dx) % side) * 2 + (core + dc) % 2

    def source(step):
        dz, dx, dc = step // (2 * side), (step // 2) % side, step % 2
        return (
            ((z + side - dz) % side) * side + (x + side - dx) % side
        ) * 2 + (core + 2 - dc) % 2

    barrier = pltpu.get_barrier_semaphore()

    def greet(step, carry):
        pl.semaphore_signal(barrier, inc=1, device_id=(to(step), grp), device_id_type=MESH)
        return carry

    lax.fori_loop(1, shards, greet, 0)
    for step in range(1, groups):
        pl.semaphore_signal(
            barrier, inc=1, device_id=(me, (grp + step) % groups), device_id_type=MESH
        )
    rows_ref[grp] = layer_norm(states_ref[...].astype(jnp.float32), norm_gain_ref[...]).astype(
        jnp.bfloat16
    )
    pl.semaphore_wait(barrier, shards + groups - 2)

    def along_grp(step, src, dst, send_sem, recv_sem):
        return pltpu.make_async_remote_copy(
            src_ref=src, dst_ref=dst, send_sem=send_sem, recv_sem=recv_sem,
            device_id=(me, (grp + step) % groups), device_id_type=MESH,
        )

    left, right, across = (grp + groups - 1) % groups, (grp + 1) % groups, (grp + 2) % groups

    def spread_grp(view, send_sem, recv_sem):
        def copy(j, incoming):
            slot = ((left, right, across, across) if incoming else (grp, grp, left, right))[j]
            place = view(slot, None if j < 2 else j - 2)
            return pltpu.make_async_remote_copy(
                src_ref=place, dst_ref=place, send_sem=send_sem(j), recv_sem=recv_sem(j),
                device_id=(me, left if j % 2 else right), device_id_type=MESH,
            )

        return copy

    def rows_view(ref):
        half = tok_rows // 2
        return lambda slot, part: (
            ref.at[slot] if part is None else ref.at[slot, pl.ds(part * half, half)]
        )

    rows_copy = spread_grp(
        rows_view(rows_ref), lambda j: rows_send.at[j], lambda j: rows_recv.at[j]
    )
    dout_copy = spread_grp(rows_view(douts), lambda j: dout_send.at[j], lambda j: dout_recv.at[j])

    def docs_copies(c):
        half = span // 2
        return spread_grp(
            lambda slot, part: (
                docs.at[slot, pl.ds(c * span, span)]
                if part is None
                else docs.at[slot, pl.ds(c * span + part * half, half)]
            ),
            lambda j: docs_send.at[c, j],
            lambda j: docs_recv.at[c, j],
        )

    def docs_own(c):
        copy = docs_copies(c)
        copy(0, False).start()
        copy(1, False).start()

    def docs_forward(c):
        copy = docs_copies(c)
        for j in range(2):
            copy(j, True).wait_recv()
            copy(j + 2, False).start()

    def sum_ring(n, lower, upper, view, tmp, into):
        def copy(j):
            src = (view(2, 0), view(2, 1), view(3, None), view(1, None))[j]
            return pltpu.make_async_remote_copy(
                src_ref=src, dst_ref=(tmp.at[j] if j < 2 else into.at[j - 2]),
                send_sem=ring_send.at[n, j], recv_sem=ring_recv.at[n, j],
                device_id=upper if j % 2 else lower, device_id_type=MESH,
            )

        def start():
            copy(0).start()
            copy(1).start()

        def middle():
            for j in range(2):
                copy(j).wait_recv()
                place = view(1 if j else 3, j)
                place[...] = (
                    place[...].astype(jnp.float32) + tmp[j].astype(jnp.float32)
                ).astype(jnp.bfloat16)
                copy(j + 2).start()

        def end():
            copy(2).wait_recv()
            copy(3).wait_recv()
            return into[0].astype(jnp.float32) + into[1].astype(jnp.float32)

        def sent():
            for j in range(4):
                copy(j).wait_send()

        return start, middle, end, sent

    def part_view(k, half):
        slot = (grp + k) % groups
        rows = tok_rows // 2
        return part.at[slot] if half is None else part.at[slot, pl.ds(half * rows, rows)]

    part_start, part_middle, part_end, part_sent = sum_ring(
        0, (me, left), (me, right), part_view, part_tmp, part_in
    )

    def along_shard(step, src, dst, send_sems, recv_sems):
        return pltpu.make_async_remote_copy(
            src_ref=src, dst_ref=dst, send_sem=send_sems.at[step], recv_sem=recv_sems.at[step],
            device_id=(to(step), grp), device_id_type=MESH,
        )

    def asks_copy(step, slot):
        return along_shard(step, tables_ref.at[to(step)], asks.at[slot], asks_send, asks_recv)

    chips = side * side
    chip = me // 2

    def chip_to(step):
        return ((z + step // side) % side) * side + (x + step % side) % side

    def chip_from(step):
        return ((z + side - step // side) % side) * side + (x + side - step % side) % side

    def query_copy(step, slot):
        return pltpu.make_async_remote_copy(
            src_ref=queries.at[chip, core], dst_ref=queries.at[slot, core],
            send_sem=chip_send.at[1, step - 1], recv_sem=chip_recv.at[1, step - 1],
            device_id=(chip_to(step) * 2 + core, grp), device_id_type=MESH,
        )

    def swap(src, dst, i):
        return pltpu.make_async_remote_copy(
            src_ref=src, dst_ref=dst, send_sem=twin_send.at[i], recv_sem=twin_recv.at[i],
            device_id=(chip * 2 + 1 - core, grp), device_id_type=MESH,
        )

    def query_swap(of):
        return swap(queries.at[:, of], queries.at[:, of], side + 1)

    def back(step, src, dst, send_sems, recv_sems):
        return pltpu.make_async_remote_copy(
            src_ref=src, dst_ref=dst, send_sem=send_sems.at[step], recv_sem=recv_sems.at[step],
            device_id=(source(step), grp), device_id_type=MESH,
        )

    def pull_copy(step, slot):
        return back(step, pull_out.at[source(step)], pull_ref.at[slot], pull_send, pull_recv)

    def score_copy(step, slot):
        return back(step, score_out.at[source(step)], score_ref.at[slot], score_send, score_recv)

    rows_copy(0, False).start()
    rows_copy(1, False).start()

    def ask(step, carry):
        asks_copy(step, me).start()
        return carry

    lax.fori_loop(1, shards, ask, 0)
    asks[me] = tables_ref[me]
    for j in range(2):
        rows_copy(j, True).wait_recv()
        rows_copy(j + 2, False).start()
    for copy in table_copies:
        copy.wait()

    def feed_forward():
        rows_copy(2, True).wait_recv()
        rows_copy(3, True).wait_recv()
        for copy in weight_copies:
            copy.wait()

        def block(r, carry):
            normed = rows_ref[r]
            gate = dot_t(normed, gate_w[...])
            up = dot_t(normed, up_w[...])
            cdf = 0.5 * (1.0 + lax.erf(gate * (1.0 / math.sqrt(2.0))))
            gelu = gate * cdf
            bell = jnp.exp(-0.5 * gate * gate) * (1.0 / math.sqrt(2.0 * math.pi))
            slope_ref[r] = ((cdf + gate * bell) * up).astype(jnp.bfloat16)
            gelu_ref[r] = gelu.astype(jnp.bfloat16)
            hidden = (gelu * up).astype(jnp.bfloat16)
            hidden_ref[r] = hidden
            down = jnp.dot(hidden, down_w[...], preferred_element_type=jnp.float32)
            part[r] = down.astype(jnp.bfloat16)

            @pl.when(r == grp)
            def _():
                part_own[...] = down

            return carry

        lax.fori_loop(0, groups, block, 0)
        part_start()

    def make_queries():
        out = states_ref[...].astype(jnp.float32) + part_own[...] + part_end()
        out_ref[...] = out
        final = layer_norm(out, final_gain_ref[...]).astype(jnp.bfloat16)
        final_t[...] = final.T
        proj = jnp.dot(final, proj_w[...], preferred_element_type=jnp.float32)
        proj_ref[...] = proj
        scale = lax.rsqrt(jnp.mean(proj * proj, axis=-1, keepdims=True) + 1e-06) / math.sqrt(dim)
        queries[chip, core] = (proj * scale).astype(jnp.bfloat16).reshape(tok_rows // q_len, q_len, dim)

        def tell(step, carry):
            query_copy(step, chip).start()
            return carry

        lax.fori_loop(1, chips, tell, 0)

    def chunk_of(c, carry):
        def passage(i, carry):
            p = c * span + 2 * i
            both = [
                rebuild_passage(p + n, blk_ref, lane_ref, codes_ref, bucket_ref, tab)
                for n in range(2)
            ]
            for n in range(2):
                docs[grp, p + n] = both[n]
            return carry

        lax.fori_loop(0, span // 2, passage, 0)
        docs_own(c)
        pl.when(c > 0)(lambda: docs_forward(c - 1))
        pl.when(c == 0)(feed_forward)
        pl.when(c == 1)(part_middle)
        pl.when(c == 3)(make_queries)
        return carry

    lax.fori_loop(0, chunks, chunk_of, 0)

    docs_forward(chunks - 1)

    def queries_in(step, carry):
        query_copy(step, chip_from(step)).wait_recv()
        return carry

    lax.fori_loop(1, chips, queries_in, 0)
    query_swap(core).start()

    def gather_in(step, carry):
        asks_copy(step, source(step)).wait_recv()
        return carry

    lax.fori_loop(1, shards, gather_in, 0)
    to_smem = pltpu.make_async_copy(asks, asks_smem, asks_sem)
    to_smem.start()
    to_smem.wait()

    query_swap(1 - core).wait_recv()

    def docs_in(c, carry):
        docs_copies(c)(2, True).wait_recv()
        docs_copies(c)(3, True).wait_recv()
        return carry

    lax.fori_loop(0, chunks, docs_in, 0)

    def answer(d):
        found = []
        for k in range(caps):
            p = asks_smem[d, 0, k]
            raw = jnp.concatenate([docs[g, p] for g in range(groups)], axis=0)
            unit = queries[d // 2, d % 2, asks_smem[d, 0, caps + k]]
            found.append(pair(raw, unit, lens_ref[p]))
        return found

    def serve(i, carry):
        found = [answer(source(2 * i + n)) for n in range(2)]
        for n in range(2):
            d = source(2 * i + n)
            for k in range(caps):
                pull_out[d, k] = found[n][k][0]
            rows = [jnp.broadcast_to(found[n][k][1], (1, dim)) for k in range(caps)]
            score_out[d] = jnp.concatenate(
                rows + [jnp.zeros((8 - caps, dim), jnp.float32)], axis=0
            )
        for n in range(2):

            @pl.when(2 * i + n > 0)
            def _():
                pull_copy(2 * i + n, me).start()
                score_copy(2 * i + n, me).start()

        @pl.when(i == 0)
        def _():
            pull_ref[me] = pull_out[me]
            score_ref[me] = score_out[me]

        return carry

    lax.fori_loop(0, shards // 2, serve, 0)

    for r in range(groups):
        turned = rows_ref[r].T.reshape(side * side, 2, rows_t.shape[2], tok_rows)
        rows_t[:, :, :, r * tok_rows : (r + 1) * tok_rows] = turned

    def finish(step, carry):
        pull_copy(step, to(step)).wait_recv()
        score_copy(step, to(step)).wait_recv()
        return carry

    lax.fori_loop(1, shards, finish, 0)

    which = which_ref[...]
    scores = 10.0 * score_ref[...].reshape(which.shape)
    top = jnp.max(jnp.where(which > 0, scores, -1e30), axis=0, keepdims=True)
    raised = jnp.where(which > 0, jnp.exp(scores - top), 0.0)
    total = jnp.sum(raised, axis=0, keepdims=True)
    chosen = jnp.sum(jnp.where(which == 2, scores, 0.0), axis=0, keepdims=True)
    loss_ref[...] = jnp.broadcast_to(top + jnp.log(total) - chosen, loss_ref.shape)
    spread = 10.0 * (raised / total - jnp.where(which == 2, 1.0, 0.0))
    q_dev = tok_rows // q_len
    for q in range(q_dev):
        weights[q] = jnp.broadcast_to(spread[:, q : q + 1], spread.shape).reshape(
            weights.shape[1:]
        )

    def gather_pull(s, sums):
        sums = list(sums)
        for k in range(caps):
            term = pull_ref[s, k].astype(jnp.float32)
            for q in range(q_dev):
                sums[q] = sums[q] + weights[q, s, k : k + 1, :] * term
        return tuple(sums)

    zero = jnp.zeros((q_len, dim), jnp.float32)
    sums = lax.fori_loop(0, shards, gather_pull, (zero,) * q_dev)
    dqueries = jnp.concatenate(sums, axis=0).astype(jnp.bfloat16).astype(jnp.float32)
    proj = proj_ref[...]
    length = lax.rsqrt(jnp.mean(proj * proj, axis=-1, keepdims=True) + 1e-06)
    along = jnp.mean(dqueries * proj, axis=-1, keepdims=True)
    dproj = (
        (length / math.sqrt(dim)) * (dqueries - proj * (length * length * along))
    ).astype(jnp.bfloat16)

    dfinal = dot_t(dproj, proj_w[...]) * final_gain_ref[...]
    out = out_ref[...]
    centre = out - jnp.mean(out, axis=-1, keepdims=True)
    inverse = lax.rsqrt(jnp.mean(centre * centre, axis=-1, keepdims=True) + 1e-05)
    unit = centre * inverse
    dout = inverse * (
        dfinal
        - jnp.mean(dfinal, axis=-1, keepdims=True)
        - unit * jnp.mean(dfinal * unit, axis=-1, keepdims=True)
    )
    douts[grp] = dout.astype(jnp.bfloat16)

    dout_copy(0, False).start()
    dout_copy(1, False).start()

    block = rows_t.shape[2]

    def chip_copy(step):
        return pltpu.make_async_remote_copy(
            src_ref=held_proj.at[chip_to(step)], dst_ref=land_proj.at[step - 1],
            send_sem=chip_send.at[0, step - 1], recv_sem=chip_recv.at[0, step - 1],
            device_id=(chip_to(step) * 2 + core, grp), device_id_type=MESH,
        )

    proj_term[...] = jnp.dot(
        final_t[...], dproj, preferred_element_type=jnp.float32
    ).reshape(proj_term.shape)
    proj_swap = swap(proj_term.at[:, 1 - core], twin_proj, side)
    proj_swap.start()

    def spread_back(i, carry):
        @pl.when(i == 1)
        def _():
            for j in range(2):
                dout_copy(j, True).wait_recv()
                dout_copy(j + 2, False).start()

        @pl.when(i == 3)
        def _():
            dout_copy(2, True).wait_recv()
            dout_copy(3, True).wait_recv()

        r = (grp + i + i // 2 - 2 * (i // 3)) % groups
        dhid = dot_t(douts[r], down_w[...])
        dgate[r] = (dhid * slope_ref[r].astype(jnp.float32)).astype(jnp.bfloat16)
        dup[r] = (dhid * gelu_ref[r].astype(jnp.float32)).astype(jnp.bfloat16)
        return carry

    lax.fori_loop(0, groups, spread_back, 0)
    for r in range(groups):
        turned = douts[r].T.reshape(chips, 2, block, tok_rows)
        douts_t[:, :, :, r * tok_rows : (r + 1) * tok_rows] = turned

    proj_swap.wait_recv()

    def add_proj(c, carry):
        held_proj[c] = proj_term[c, core] + twin_proj[c]
        return carry

    lax.fori_loop(0, chips, add_proj, 0)

    def send_proj(step, carry):
        chip_copy(step).start()
        return carry

    lax.fori_loop(1, chips, send_proj, 0)

    tokens = groups * tok_rows

    main = gate_out.shape[1] // 128 * 128
    rest = gate_out.shape[1] - main

    def terms(row, half):
        found = []
        for lhs, rhs in ((rows_t, dgate), (rows_t, dup), (douts_t, hidden_ref)):
            found.append(
                jnp.dot(
                    lhs[pl.ds(row * side, side), half].reshape(side * block, tokens),
                    rhs[...].reshape(tokens, main + rest),
                    preferred_element_type=jnp.float32,
                )
            )
        fill = jnp.zeros((side * block, held.shape[3] - 3 * (main + rest)), jnp.float32)
        return jnp.concatenate(
            [t[:, :main] for t in found] + [t[:, main:] for t in found] + [fill], axis=1
        ).reshape(side, block, held.shape[3])

    def row_of(i):
        return (z + 2 + i) % side

    def swap_copy(i):
        return swap(first.at[row_of(i)], twin.at[row_of(i)], i)

    def give(i, carry):
        first[row_of(i)] = terms(row_of(i), 1 - core).astype(jnp.bfloat16)
        swap_copy(i).start()
        return carry

    lax.fori_loop(0, side, give, 0)

    cols = held.shape[3] // 2
    few = side // 2
    x_low = ((z * side + (x + side - 1) % side) * 2 + core, grp)
    x_high = ((z * side + (x + 1) % side) * 2 + core, grp)
    z_low = ((((z + side - 1) % side) * side + x) * 2 + core, grp)
    z_high = ((((z + 1) % side) * side + x) * 2 + core, grp)

    def view_x(k, half):
        rows = pl.ds(0, side) if half is None else pl.ds(half * few, few)
        return held.at[rows, (x + k) % side, :, pl.ds(0, cols)]

    def view_z(k, half):
        rows = pl.ds(0, side) if half is None else pl.ds(half * few, few)
        return held.at[(z + k) % side, rows, :, pl.ds(cols, cols)]

    def view_mid(n, place):
        def view(k, half):
            spot = (place + k) % side
            part = block // 2
            return mids.at[n, spot] if half is None else mids.at[n, spot, pl.ds(half * part, part)]

        return view

    ring_x = sum_ring(1, x_low, x_high, view_x, tmp_one.at[0], in_one.at[0])
    ring_z = sum_ring(2, z_low, z_high, view_z, tmp_one.at[1], in_one.at[1])
    then_z = sum_ring(3, z_low, z_high, view_mid(0, z), tmp_two.at[0], in_two.at[0])
    then_x = sum_ring(4, x_low, x_high, view_mid(1, x), tmp_two.at[1], in_two.at[1])

    def keep(i, carry):
        swap_copy(i).wait_recv()
        held[row_of(i)] = (
            terms(row_of(i), core) + twin[row_of(i)].astype(jnp.float32)
        ).astype(jnp.bfloat16)
        pl.when(i == 0)(ring_z[0])
        return carry

    lax.fori_loop(0, side, keep, 0)
    ring_x[0]()
    ring_z[1]()
    ring_x[1]()

    def proj_in(step, total):
        chip_copy(step).wait_recv()
        return total + land_proj[step - 1]

    rows_sum[...] = lax.fori_loop(1, chips, proj_in, held_proj[chip]).reshape(rows_sum.shape)

    def sum_copy(step):
        return along_grp(
            step, rows_sum.at[(grp + step) % groups], land_grp.at[step - 1],
            grp_send.at[step], grp_recv.at[step],
        )

    for step in range(1, groups):
        sum_copy(step).start()
    mine = rows_sum[grp]
    for step in range(1, groups):
        sum_copy(step).wait_recv()
        mine = mine + land_grp[step - 1]
    proj_out[...] = mine

    mids[1] = (view_z(0, None)[...].astype(jnp.float32) + ring_z[2]()).astype(jnp.bfloat16)
    then_x[0]()
    mids[0] = (view_x(0, None)[...].astype(jnp.float32) + ring_x[2]()).astype(jnp.bfloat16)
    then_z[0]()
    then_x[1]()
    then_z[1]()
    whole = jnp.concatenate(
        [
            mids[0, z].astype(jnp.float32) + then_z[2](),
            mids[1, x].astype(jnp.float32) + then_x[2](),
        ],
        axis=1,
    )
    for n, ref in enumerate((gate_out, up_out, down_out)):
        ref[:, :main] = whole[:, n * main : (n + 1) * main]
        ref[:, main:] = whole[:, 3 * main + n * rest : 3 * main + (n + 1) * rest]

    def sent(step, carry):
        asks_copy(step, me).wait_send()
        pull_copy(step, me).wait_send()
        score_copy(step, me).wait_send()
        return carry

    lax.fori_loop(1, shards, sent, 0)
    for step in range(1, groups):
        sum_copy(step).wait_send()
    for j in range(4):
        rows_copy(j, False).wait_send()
        dout_copy(j, False).wait_send()
    for ring in (ring_x, ring_z, then_x, then_z):
        ring[3]()
    part_sent()
    query_swap(core).wait_send()

    def docs_out(c, carry):
        for j in range(4):
            docs_copies(c)(j, False).wait_send()
        return carry

    lax.fori_loop(0, chunks, docs_out, 0)
    proj_swap.wait_send()

    def swapped(i, carry):
        swap_copy(i).wait_send()
        return carry

    lax.fori_loop(0, side, swapped, 0)

    def chips_out(step, carry):
        chip_copy(step).wait_send()
        query_copy(step, chip).wait_send()
        return carry

    lax.fori_loop(1, chips, chips_out, 0)


def step_call(
    states, norm_gain, final_gain, w_gate, w_up, w_down_t, w_proj, cent_ids, lens, codes, bucket,
    tables, which, table, side, caps, q_len,
):
    groups = lax.axis_size("grp")
    shards = 2 * side * side
    chips = side * side
    tok_rows, width = states.shape
    part = w_gate.shape[0]
    dim = w_proj.shape[1]
    passages, toks = cent_ids.shape
    dims, count = table.shape
    chunks = 8
    block = width // shards
    tokens = groups * tok_rows
    spread = jnp.broadcast_to(bucket[:, :, None], (4, dims, toks))
    vmem = pl.BlockSpec(memory_space=pltpu.VMEM)
    smem = pl.BlockSpec(memory_space=pltpu.SMEM)
    hbm = pl.BlockSpec(memory_space=pl.ANY)
    bf16, f32 = jnp.bfloat16, jnp.float32
    dma = pltpu.SemaphoreType.DMA
    wide = (side, side, block, -(-3 * part // 256) * 256)
    cols = wide[3] // 2
    return pl.pallas_call(
        functools.partial(step_kernel, side, groups, chunks),
        out_shape=(jax.ShapeDtypeStruct((8, 128), f32),)
        + (jax.ShapeDtypeStruct((block, part), f32),) * 3
        + (jax.ShapeDtypeStruct((block // groups, dim), f32),),
        in_specs=[vmem] * 3 + [hbm] * 3 + [vmem] + [smem] * 2 + [vmem] * 5 + [hbm],
        out_specs=(vmem,) * 5,
        scratch_shapes=[
            pltpu.VMEM((dims, count), bf16),
            pltpu.VMEM((part, width), bf16),
            pltpu.VMEM((part, width), bf16),
            pltpu.VMEM((part, width), bf16),
            pltpu.VMEM((groups, passages, dims, toks), bf16),
            pltpu.VMEM((groups, tok_rows, width), bf16),
            pltpu.VMEM((groups, tok_rows, part), bf16),
            pltpu.VMEM((groups, tok_rows, part), bf16),
            pltpu.VMEM((groups, tok_rows, part), bf16),
            pltpu.VMEM((groups, tok_rows, width), bf16),
            pltpu.VMEM((tok_rows, width), f32),
            pltpu.VMEM((2, tok_rows // 2, width), bf16),
            pltpu.VMEM((2, tok_rows, width), bf16),
            pltpu.VMEM((tok_rows, width), f32),
            pltpu.VMEM((width, tok_rows), bf16),
            pltpu.VMEM((tok_rows, dim), f32),
            pltpu.VMEM((shards, 1, 128), jnp.int32),
            pltpu.SMEM((shards, 1, 128), jnp.int32),
            pltpu.VMEM((chips, 2, tok_rows // q_len, q_len, dim), bf16),
            pltpu.VMEM((shards, caps, q_len, dim), bf16),
            pltpu.VMEM((shards, 8, dim), f32),
            pltpu.VMEM((shards, caps, q_len, dim), bf16),
            pltpu.VMEM((shards, 8, dim), f32),
            pltpu.VMEM((tok_rows // q_len, shards, 8, dim), f32),
            pltpu.VMEM((groups, tok_rows, width), bf16),
            pltpu.VMEM((chips, 2, block, tokens), bf16),
            pltpu.VMEM((chips, 2, block, tokens), bf16),
            pltpu.VMEM((groups, tok_rows, part), bf16),
            pltpu.VMEM((groups, tok_rows, part), bf16),
            pltpu.VMEM(wide, bf16),
            pltpu.VMEM(wide, bf16),
            pltpu.VMEM(wide, bf16),
            pltpu.VMEM((2, 2, side // 2, block, cols), bf16),
            pltpu.VMEM((2, 2, side, block, cols), bf16),
            pltpu.VMEM((2, side, block, cols), bf16),
            pltpu.VMEM((2, 2, block // 2, cols), bf16),
            pltpu.VMEM((2, 2, block, cols), bf16),
            pltpu.VMEM((chips, 2, block, dim), f32),
            pltpu.VMEM((chips, block, dim), f32),
            pltpu.VMEM((chips, block, dim), f32),
            pltpu.VMEM((chips - 1, block, dim), f32),
            pltpu.VMEM((groups, block // groups, dim), f32),
            pltpu.VMEM((groups - 1, block // groups, dim), f32),
            dma((8,)),
            dma((3,)),
            dma,
        ]
        + [dma((groups,))] * 6
        + [dma((chunks, groups))] * 2
        + [dma((5, groups))] * 2
        + [dma((shards,))] * 6
        + [dma((side + 2,))] * 2
        + [dma((2, chips - 1))] * 2,
        compiler_params=pltpu.CompilerParams(
            collective_id=0, has_side_effects=True, vmem_limit_bytes=60 << 20
        ),
        cost_estimate=pl.CostEstimate(flops=0, bytes_accessed=300_000_000, transcendentals=0),
    )(
        states, norm_gain, final_gain, w_gate, w_up, w_down_t, w_proj, cent_ids >> 7, lens,
        cent_ids & 127, codes, spread, tables, which, table,
    )


def coords(shape):
    me = lax.axis_index("shard")
    return me // (2 * shape), (me // 2) % shape, me % 2, lax.axis_index("grp")


def ranks(hits):
    count = hits.shape[1]
    before = lax.broadcasted_iota(jnp.int32, (count, count), 0) < lax.broadcasted_iota(
        jnp.int32, (count, count), 1
    )
    return jnp.dot(
        hits.astype(jnp.bfloat16), before.astype(jnp.bfloat16), preferred_element_type=jnp.float32
    ).astype(jnp.int32)


def slots(hits, caps):
    nth = lax.broadcasted_iota(jnp.int32, (1, caps, 1), 1)
    return hits[:, None, :] & (ranks(hits)[:, None, :] == nth)


def local(
    query_states,
    norm_gain,
    final_gain,
    w_gate,
    w_up,
    w_down_t,
    w_proj,
    centroids,
    bucket_values,
    centroid_ids,
    residual_codes,
    passage_lens,
    negative_ids,
):
    q_dev, q_len, width = query_states.shape
    dim = w_proj.shape[1]
    shards = lax.axis_size("shard")
    side = math.isqrt(shards // 2)
    cands = negative_ids.shape[1]
    tok_rows = q_dev * q_len
    local_pass = centroid_ids.shape[0]
    caps = 2 * q_dev * cands // shards
    me = lax.axis_index("shard")

    flat_ids = negative_ids.reshape(1, -1)
    owner = lax.broadcasted_iota(jnp.int32, (shards, 1), 0)
    places = lax.broadcasted_iota(jnp.int32, (1, 1, q_dev * cands), 2)
    sent = slots(flat_ids // local_pass == owner, caps)
    place = jnp.sum(jnp.where(sent, places, 0), axis=2)
    asked = jnp.sum(jnp.where(sent, (flat_ids % local_pass)[:, None, :], 0), axis=2)
    tables = jnp.concatenate(
        [asked, place // cands, jnp.zeros((shards, 128 - 2 * caps), jnp.int32)], axis=1
    ).reshape(shards, 1, 128)
    lens = lax.dynamic_slice(passage_lens, (me * local_pass,), (local_pass,))
    states = query_states.reshape(tok_rows, width)
    filled = jnp.any(sent, axis=2)[:, :, None]
    query = lax.broadcasted_iota(jnp.int32, (1, 1, 128), 2)
    mine = filled & ((place // cands)[:, :, None] == query)
    first = mine & ((place % cands)[:, :, None] == 0)
    which = mine.astype(jnp.int32) + first.astype(jnp.int32)
    which = jnp.pad(which, ((0, 0), (0, 8 - caps), (0, 0))).reshape(shards * 8, 128)
    losses, grad_gate, grad_up, grad_down, grad_proj = step_call(
        states, norm_gain.reshape(1, -1), final_gain.reshape(1, -1), w_gate.T, w_up.T, w_down_t.T,
        w_proj, centroid_ids, lens, residual_codes, bucket_values, tables, which, centroids, side,
        caps, q_len,
    )
    return (losses[0, :q_dev], grad_gate, grad_up, grad_down, grad_proj)


def solution(mesh):
    placed = (
        P(("shard", "grp"), None, None),
        P(),
        P(),
        P(None, "grp"),
        P(None, "grp"),
        P(None, "grp"),
        P(),
        P("grp", None),
        P(None, "grp"),
        P("shard", None),
        P("shard", "grp", None),
        P(),
        P(("shard", "grp"), None),
    )
    return jax.shard_map(
        local,
        mesh=mesh,
        in_specs=placed,
        out_specs=(
            P(("shard", "grp")),
            P("shard", "grp"),
            P("shard", "grp"),
            P("shard", "grp"),
            P(("shard", "grp"), None),
        ),
        check_vma=False,
    )
```

```python
import functools
import math

import jax
import jax.numpy as jnp
from jax import lax
from jax.experimental import pallas as pl
from jax.experimental.pallas import tpu as pltpu
from jax.sharding import PartitionSpec as P

MESH = pl.DeviceIdType.MESH


def layer_norm(rows, gain):
    centre = rows - jnp.mean(rows, axis=-1, keepdims=True)
    spread = jnp.mean(centre * centre, axis=-1, keepdims=True)
    return centre * lax.rsqrt(spread + 1e-05) * gain


def rebuild_passage(p, blk_ref, lane_ref, codes_ref, bucket_ref, tab):
    dims, toks = tab.shape[0], lane_ref.shape[1]
    lane = lax.broadcasted_iota(jnp.int32, (dims, toks), 1)
    shift = 2 * lax.broadcasted_iota(jnp.int32, (8, toks), 0)
    spot = jnp.broadcast_to(jnp.bitwise_and(lane_ref[pl.ds(p, 1), :], 127), (dims, toks))
    base = jnp.zeros((dims, toks), jnp.float32)
    for j in range(toks):
        block = tab[:, pl.ds(blk_ref[p, j] * 128, 128)].astype(jnp.float32)
        near = jnp.take_along_axis(block, spot, axis=1, mode="promise_in_bounds")
        base = jnp.where(lane == j, near, base)
    words = codes_ref[p]
    fields = jnp.concatenate(
        [
            jnp.bitwise_and(
                jnp.right_shift(jnp.broadcast_to(words[w : w + 1], (8, toks)), shift), 3
            )
            for w in range(dims // 8)
        ],
        axis=0,
    )
    resid = jnp.where(
        fields < 2,
        jnp.where(fields == 0, bucket_ref[0], bucket_ref[1]),
        jnp.where(fields == 2, bucket_ref[2], bucket_ref[3]),
    )
    return (base + resid).astype(jnp.bfloat16)


def dot_t(left, right):
    return lax.dot_general(
        left, right, (((1,), (1,)), ((), ())), preferred_element_type=jnp.float32
    )


def pair(docs, queries, count):
    q_len, dim = queries.shape
    toks = docs.shape[1]
    spots = lax.broadcasted_iota(jnp.int32, (q_len, toks), 1)
    values = docs.astype(jnp.float32)
    scale = lax.rsqrt(jnp.mean(values * values, axis=0, keepdims=True) + 1e-06) / math.sqrt(dim)
    sims = jnp.dot(queries, docs, preferred_element_type=jnp.float32)
    raised = jnp.where(spots < count, jnp.exp(64.0 * (sims * scale)), 0.0)
    total = jnp.sum(raised, axis=1, keepdims=True)
    score = jnp.sum(jnp.log(total), axis=0, keepdims=True) / 64.0
    pull = dot_t((raised * (scale / total)).astype(jnp.bfloat16), docs)
    return pull.astype(jnp.bfloat16), score


def step_kernel(
    side, groups, chunks,
    states_ref, norm_gain_ref, final_gain_ref, gate_hbm, up_hbm, down_hbm, proj_w,
    blk_ref, lens_ref, lane_ref, codes_ref, levels_ref, tables_ref, which_ref, tab_hbm,
    loss_ref, gate_out, up_out, down_out, proj_out,
    tab, bucket_ref, gate_w, up_w, down_w, docs, rows_ref, slope_ref, gelu_ref, hidden_ref, part, part_own, part_tmp, part_in, out_ref,
    final_t, proj_ref, asks, asks_smem, queries, pull_out, score_out, pull_ref, score_ref,
    weights, douts, rows_t, douts_t, dgate, dup, first, twin, held,
    tmp_one, in_one, mids, tmp_two, in_two,
    proj_term, twin_proj, held_proj, land_proj, rows_sum, land_grp,
    tab_sem, weight_sem, asks_sem, rows_send, rows_recv, dout_send, dout_recv,
    grp_send, grp_recv, docs_send, docs_recv, ring_send, ring_recv,
    asks_send, asks_recv, pull_send, pull_recv, score_send, score_recv,
    twin_send, twin_recv, chip_send, chip_recv,
):
    z, x, core, grp = coords(side)
    me = (z * side + x) * 2 + core
    shards = 2 * side * side
    passages, toks = lane_ref.shape
    span = passages // chunks
    tok_rows = states_ref.shape[0]
    caps, q_len, dim = pull_ref.shape[1:]

    pieces = tab_sem.shape[0]
    width = tab.shape[1] // pieces
    table_copies = [
        pltpu.make_async_copy(
            tab_hbm.at[:, pl.ds(i * width, width)], tab.at[:, pl.ds(i * width, width)], tab_sem.at[i]
        )
        for i in range(pieces)
    ]
    weight_copies = [
        pltpu.make_async_copy(src, dst, weight_sem.at[n])
        for n, (src, dst) in enumerate(((gate_hbm, gate_w), (up_hbm, up_w), (down_hbm, down_w)))
    ]
    for copy in table_copies + weight_copies:
        copy.start()

    def to(step):
        dz, dx, dc = step // (2 * side), (step // 2) % side, step % 2
        return (((z + dz) % side) * side + (x + dx) % side) * 2 + (core + dc) % 2

    def source(step):
        dz, dx, dc = step // (2 * side), (step // 2) % side, step % 2
        return (
            ((z + side - dz) % side) * side + (x + side - dx) % side
        ) * 2 + (core + 2 - dc) % 2

    for level in range(4):
        row = levels_ref[level : level + 1, :]
        bucket_ref[level] = jnp.broadcast_to(row, (toks, row.shape[1])).T
    barrier = pltpu.get_barrier_semaphore()

    def greet(step, carry):
        pl.semaphore_signal(barrier, inc=1, device_id=(to(step), grp), device_id_type=MESH)
        return carry

    lax.fori_loop(1, shards, greet, 0)
    for step in range(1, groups):
        pl.semaphore_signal(
            barrier, inc=1, device_id=(me, (grp + step) % groups), device_id_type=MESH
        )
    rows_ref[grp] = layer_norm(states_ref[...].astype(jnp.float32), norm_gain_ref[...]).astype(
        jnp.bfloat16
    )
    pl.semaphore_wait(barrier, shards + groups - 2)

    def along_grp(step, src, dst, send_sem, recv_sem):
        return pltpu.make_async_remote_copy(
            src_ref=src, dst_ref=dst, send_sem=send_sem, recv_sem=recv_sem,
            device_id=(me, (grp + step) % groups), device_id_type=MESH,
        )

    left, right, across = (grp + groups - 1) % groups, (grp + 1) % groups, (grp + 2) % groups

    def spread_grp(view, send_sem, recv_sem):
        def copy(j, incoming):
            slot = ((left, right, across, across) if incoming else (grp, grp, left, right))[j]
            place = view(slot, None if j < 2 else j - 2)
            return pltpu.make_async_remote_copy(
                src_ref=place, dst_ref=place, send_sem=send_sem(j), recv_sem=recv_sem(j),
                device_id=(me, left if j % 2 else right), device_id_type=MESH,
            )

        return copy

    def rows_view(ref):
        half = tok_rows // 2
        return lambda slot, part: (
            ref.at[slot] if part is None else ref.at[slot, pl.ds(part * half, half)]
        )

    rows_copy = spread_grp(
        rows_view(rows_ref), lambda j: rows_send.at[j], lambda j: rows_recv.at[j]
    )
    dout_copy = spread_grp(rows_view(douts), lambda j: dout_send.at[j], lambda j: dout_recv.at[j])

    def docs_copies(c):
        half = span // 2
        return spread_grp(
            lambda slot, part: (
                docs.at[slot, pl.ds(c * span, span)]
                if part is None
                else docs.at[slot, pl.ds(c * span + part * half, half)]
            ),
            lambda j: docs_send.at[c, j],
            lambda j: docs_recv.at[c, j],
        )

    def docs_own(c):
        copy = docs_copies(c)
        copy(0, False).start()
        copy(1, False).start()

    def docs_forward(c):
        copy = docs_copies(c)
        for j in range(2):
            copy(j, True).wait_recv()
            copy(j + 2, False).start()

    def sum_ring(n, lower, upper, view, tmp, into):
        def copy(j):
            src = (view(2, 0), view(2, 1), view(3, None), view(1, None))[j]
            return pltpu.make_async_remote_copy(
                src_ref=src, dst_ref=(tmp.at[j] if j < 2 else into.at[j - 2]),
                send_sem=ring_send.at[n, j], recv_sem=ring_recv.at[n, j],
                device_id=upper if j % 2 else lower, device_id_type=MESH,
            )

        def start():
            copy(0).start()
            copy(1).start()

        def middle():
            for j in range(2):
                copy(j).wait_recv()
                place = view(1 if j else 3, j)
                place[...] = (
                    place[...].astype(jnp.float32) + tmp[j].astype(jnp.float32)
                ).astype(jnp.bfloat16)
                copy(j + 2).start()

        def end():
            copy(2).wait_recv()
            copy(3).wait_recv()
            return into[0].astype(jnp.float32) + into[1].astype(jnp.float32)

        def sent():
            for j in range(4):
                copy(j).wait_send()

        return start, middle, end, sent

    def part_view(k, half):
        slot = (grp + k) % groups
        rows = tok_rows // 2
        return part.at[slot] if half is None else part.at[slot, pl.ds(half * rows, rows)]

    part_start, part_middle, part_end, part_sent = sum_ring(
        0, (me, left), (me, right), part_view, part_tmp, part_in
    )

    def along_shard(step, src, dst, send_sems, recv_sems):
        return pltpu.make_async_remote_copy(
            src_ref=src, dst_ref=dst, send_sem=send_sems.at[step], recv_sem=recv_sems.at[step],
            device_id=(to(step), grp), device_id_type=MESH,
        )

    def asks_copy(step, slot):
        return along_shard(step, tables_ref.at[to(step)], asks.at[slot], asks_send, asks_recv)

    chips = side * side
    chip = me // 2

    def chip_to(step):
        return ((z + step // side) % side) * side + (x + step % side) % side

    def chip_from(step):
        return ((z + side - step // side) % side) * side + (x + side - step % side) % side

    def query_copy(step, slot):
        return pltpu.make_async_remote_copy(
            src_ref=queries.at[chip, core], dst_ref=queries.at[slot, core],
            send_sem=chip_send.at[1, step - 1], recv_sem=chip_recv.at[1, step - 1],
            device_id=(chip_to(step) * 2 + core, grp), device_id_type=MESH,
        )

    def swap(src, dst, i):
        return pltpu.make_async_remote_copy(
            src_ref=src, dst_ref=dst, send_sem=twin_send.at[i], recv_sem=twin_recv.at[i],
            device_id=(chip * 2 + 1 - core, grp), device_id_type=MESH,
        )

    def query_swap(of):
        return swap(queries.at[:, of], queries.at[:, of], side + 1)

    def back(step, src, dst, send_sems, recv_sems):
        return pltpu.make_async_remote_copy(
            src_ref=src, dst_ref=dst, send_sem=send_sems.at[step], recv_sem=recv_sems.at[step],
            device_id=(source(step), grp), device_id_type=MESH,
        )

    def pull_copy(step, slot):
        return back(step, pull_out.at[source(step)], pull_ref.at[slot], pull_send, pull_recv)

    def score_copy(step, slot):
        return back(step, score_out.at[source(step)], score_ref.at[slot], score_send, score_recv)

    rows_copy(0, False).start()
    rows_copy(1, False).start()

    def ask(step, carry):
        asks_copy(step, me).start()
        return carry

    lax.fori_loop(1, shards, ask, 0)
    asks[me] = tables_ref[me]
    for j in range(2):
        rows_copy(j, True).wait_recv()
        rows_copy(j + 2, False).start()
    for copy in table_copies:
        copy.wait()

    def feed_forward():
        rows_copy(2, True).wait_recv()
        rows_copy(3, True).wait_recv()
        for copy in weight_copies:
            copy.wait()

        def block(r, carry):
            normed = rows_ref[r]
            gate = dot_t(normed, gate_w[...])
            up = dot_t(normed, up_w[...])
            cdf = 0.5 * (1.0 + lax.erf(gate * (1.0 / math.sqrt(2.0))))
            gelu = gate * cdf
            bell = jnp.exp(-0.5 * gate * gate) * (1.0 / math.sqrt(2.0 * math.pi))
            slope_ref[r] = ((cdf + gate * bell) * up).astype(jnp.bfloat16)
            gelu_ref[r] = gelu.astype(jnp.bfloat16)
            hidden = (gelu * up).astype(jnp.bfloat16)
            hidden_ref[r] = hidden
            down = jnp.dot(hidden, down_w[...], preferred_element_type=jnp.float32)
            part[r] = down.astype(jnp.bfloat16)

            @pl.when(r == grp)
            def _():
                part_own[...] = down

            return carry

        lax.fori_loop(0, groups, block, 0)
        part_start()

    def make_queries():
        out = states_ref[...].astype(jnp.float32) + part_own[...] + part_end()
        out_ref[...] = out
        final = layer_norm(out, final_gain_ref[...]).astype(jnp.bfloat16)
        final_t[...] = final.T
        proj = jnp.dot(final, proj_w[...], preferred_element_type=jnp.float32)
        proj_ref[...] = proj
        scale = lax.rsqrt(jnp.mean(proj * proj, axis=-1, keepdims=True) + 1e-06) / math.sqrt(dim)
        queries[chip, core] = (proj * scale).astype(jnp.bfloat16).reshape(tok_rows // q_len, q_len, dim)

        def tell(step, carry):
            query_copy(step, chip).start()
            return carry

        lax.fori_loop(1, chips, tell, 0)

    def chunk_of(c, carry):
        def passage(i, carry):
            p = c * span + 2 * i
            both = [
                rebuild_passage(p + n, blk_ref, lane_ref, codes_ref, bucket_ref, tab)
                for n in range(2)
            ]
            for n in range(2):
                docs[grp, p + n] = both[n]
            return carry

        lax.fori_loop(0, span // 2, passage, 0)
        docs_own(c)
        pl.when(c > 0)(lambda: docs_forward(c - 1))
        pl.when(c == 0)(feed_forward)
        pl.when(c == 1)(part_middle)
        pl.when(c == 3)(make_queries)
        return carry

    lax.fori_loop(0, chunks, chunk_of, 0)

    docs_forward(chunks - 1)

    def queries_in(step, carry):
        query_copy(step, chip_from(step)).wait_recv()
        return carry

    lax.fori_loop(1, chips, queries_in, 0)
    query_swap(core).start()

    def gather_in(step, carry):
        asks_copy(step, source(step)).wait_recv()
        return carry

    lax.fori_loop(1, shards, gather_in, 0)
    to_smem = pltpu.make_async_copy(asks, asks_smem, asks_sem)
    to_smem.start()
    to_smem.wait()

    query_swap(1 - core).wait_recv()

    def docs_in(c, carry):
        docs_copies(c)(2, True).wait_recv()
        docs_copies(c)(3, True).wait_recv()
        return carry

    lax.fori_loop(0, chunks, docs_in, 0)

    def answer(d):
        found = []
        for k in range(caps):
            p = asks_smem[d, 0, k]
            raw = jnp.concatenate([docs[g, p] for g in range(groups)], axis=0)
            unit = queries[d // 2, d % 2, asks_smem[d, 0, caps + k]]
            found.append(pair(raw, unit, lens_ref[p]))
        return found

    def serve(i, carry):
        found = [answer(source(2 * i + n)) for n in range(2)]
        for n in range(2):
            d = source(2 * i + n)
            for k in range(caps):
                pull_out[d, k] = found[n][k][0]
            rows = [jnp.broadcast_to(found[n][k][1], (1, dim)) for k in range(caps)]
            score_out[d] = jnp.concatenate(
                rows + [jnp.zeros((8 - caps, dim), jnp.float32)], axis=0
            )
        for n in range(2):

            @pl.when(2 * i + n > 0)
            def _():
                pull_copy(2 * i + n, me).start()
                score_copy(2 * i + n, me).start()

        @pl.when(i == 0)
        def _():
            pull_ref[me] = pull_out[me]
            score_ref[me] = score_out[me]

        return carry

    lax.fori_loop(0, shards // 2, serve, 0)

    for r in range(groups):
        turned = rows_ref[r].T.reshape(side * side, 2, rows_t.shape[2], tok_rows)
        rows_t[:, :, :, r * tok_rows : (r + 1) * tok_rows] = turned

    def finish(step, carry):
        pull_copy(step, to(step)).wait_recv()
        score_copy(step, to(step)).wait_recv()
        return carry

    lax.fori_loop(1, shards, finish, 0)

    which = which_ref[...]
    scores = 10.0 * score_ref[...].reshape(which.shape)
    top = jnp.max(jnp.where(which > 0, scores, -1e30), axis=0, keepdims=True)
    raised = jnp.where(which > 0, jnp.exp(scores - top), 0.0)
    total = jnp.sum(raised, axis=0, keepdims=True)
    chosen = jnp.sum(jnp.where(which == 2, scores, 0.0), axis=0, keepdims=True)
    loss_ref[...] = jnp.broadcast_to(top + jnp.log(total) - chosen, loss_ref.shape)
    spread = 10.0 * (raised / total - jnp.where(which == 2, 1.0, 0.0))
    q_dev = tok_rows // q_len
    for q in range(q_dev):
        weights[q] = jnp.broadcast_to(spread[:, q : q + 1], spread.shape).reshape(
            weights.shape[1:]
        )

    def gather_pull(s, sums):
        sums = list(sums)
        for k in range(caps):
            term = pull_ref[s, k].astype(jnp.float32)
            for q in range(q_dev):
                sums[q] = sums[q] + weights[q, s, k : k + 1, :] * term
        return tuple(sums)

    zero = jnp.zeros((q_len, dim), jnp.float32)
    sums = lax.fori_loop(0, shards, gather_pull, (zero,) * q_dev)
    dqueries = jnp.concatenate(sums, axis=0).astype(jnp.bfloat16).astype(jnp.float32)
    proj = proj_ref[...]
    length = lax.rsqrt(jnp.mean(proj * proj, axis=-1, keepdims=True) + 1e-06)
    along = jnp.mean(dqueries * proj, axis=-1, keepdims=True)
    dproj = (
        (length / math.sqrt(dim)) * (dqueries - proj * (length * length * along))
    ).astype(jnp.bfloat16)

    dfinal = dot_t(dproj, proj_w[...]) * final_gain_ref[...]
    out = out_ref[...]
    centre = out - jnp.mean(out, axis=-1, keepdims=True)
    inverse = lax.rsqrt(jnp.mean(centre * centre, axis=-1, keepdims=True) + 1e-05)
    unit = centre * inverse
    dout = inverse * (
        dfinal
        - jnp.mean(dfinal, axis=-1, keepdims=True)
        - unit * jnp.mean(dfinal * unit, axis=-1, keepdims=True)
    )
    douts[grp] = dout.astype(jnp.bfloat16)

    dout_copy(0, False).start()
    dout_copy(1, False).start()

    block = rows_t.shape[2]

    def chip_copy(step):
        return pltpu.make_async_remote_copy(
            src_ref=held_proj.at[chip_to(step)], dst_ref=land_proj.at[step - 1],
            send_sem=chip_send.at[0, step - 1], recv_sem=chip_recv.at[0, step - 1],
            device_id=(chip_to(step) * 2 + core, grp), device_id_type=MESH,
        )

    proj_term[...] = jnp.dot(
        final_t[...], dproj, preferred_element_type=jnp.float32
    ).reshape(proj_term.shape)
    proj_swap = swap(proj_term.at[:, 1 - core], twin_proj, side)
    proj_swap.start()

    def spread_back(i, carry):
        @pl.when(i == 1)
        def _():
            for j in range(2):
                dout_copy(j, True).wait_recv()
                dout_copy(j + 2, False).start()

        @pl.when(i == 3)
        def _():
            dout_copy(2, True).wait_recv()
            dout_copy(3, True).wait_recv()

        r = (grp + i + i // 2 - 2 * (i // 3)) % groups
        dhid = dot_t(douts[r], down_w[...])
        dgate[r] = (dhid * slope_ref[r].astype(jnp.float32)).astype(jnp.bfloat16)
        dup[r] = (dhid * gelu_ref[r].astype(jnp.float32)).astype(jnp.bfloat16)
        return carry

    lax.fori_loop(0, groups, spread_back, 0)
    for r in range(groups):
        turned = douts[r].T.reshape(chips, 2, block, tok_rows)
        douts_t[:, :, :, r * tok_rows : (r + 1) * tok_rows] = turned

    proj_swap.wait_recv()

    def add_proj(c, carry):
        held_proj[c] = proj_term[c, core] + twin_proj[c]
        return carry

    lax.fori_loop(0, chips, add_proj, 0)

    def send_proj(step, carry):
        chip_copy(step).start()
        return carry

    lax.fori_loop(1, chips, send_proj, 0)

    tokens = groups * tok_rows

    main = gate_out.shape[1] // 128 * 128
    rest = gate_out.shape[1] - main

    def terms(row, half):
        found = []
        for lhs, rhs in ((rows_t, dgate), (rows_t, dup), (douts_t, hidden_ref)):
            found.append(
                jnp.dot(
                    lhs[pl.ds(row * side, side), half].reshape(side * block, tokens),
                    rhs[...].reshape(tokens, main + rest),
                    preferred_element_type=jnp.float32,
                )
            )
        fill = jnp.zeros((side * block, held.shape[3] - 3 * (main + rest)), jnp.float32)
        return jnp.concatenate(
            [t[:, :main] for t in found] + [t[:, main:] for t in found] + [fill], axis=1
        ).reshape(side, block, held.shape[3])

    def row_of(i):
        return (z + 2 + i) % side

    def swap_copy(i):
        return swap(first.at[row_of(i)], twin.at[row_of(i)], i)

    def give(i, carry):
        first[row_of(i)] = terms(row_of(i), 1 - core).astype(jnp.bfloat16)
        swap_copy(i).start()
        return carry

    lax.fori_loop(0, side, give, 0)

    cols = held.shape[3] // 2
    few = side // 2
    x_low = ((z * side + (x + side - 1) % side) * 2 + core, grp)
    x_high = ((z * side + (x + 1) % side) * 2 + core, grp)
    z_low = ((((z + side - 1) % side) * side + x) * 2 + core, grp)
    z_high = ((((z + 1) % side) * side + x) * 2 + core, grp)

    def view_x(k, half):
        rows = pl.ds(0, side) if half is None else pl.ds(half * few, few)
        return held.at[rows, (x + k) % side, :, pl.ds(0, cols)]

    def view_z(k, half):
        rows = pl.ds(0, side) if half is None else pl.ds(half * few, few)
        return held.at[(z + k) % side, rows, :, pl.ds(cols, cols)]

    def view_mid(n, place):
        def view(k, half):
            spot = (place + k) % side
            part = block // 2
            return mids.at[n, spot] if half is None else mids.at[n, spot, pl.ds(half * part, part)]

        return view

    ring_x = sum_ring(1, x_low, x_high, view_x, tmp_one.at[0], in_one.at[0])
    ring_z = sum_ring(2, z_low, z_high, view_z, tmp_one.at[1], in_one.at[1])
    then_z = sum_ring(3, z_low, z_high, view_mid(0, z), tmp_two.at[0], in_two.at[0])
    then_x = sum_ring(4, x_low, x_high, view_mid(1, x), tmp_two.at[1], in_two.at[1])

    def keep(i, carry):
        swap_copy(i).wait_recv()
        held[row_of(i)] = (
            terms(row_of(i), core) + twin[row_of(i)].astype(jnp.float32)
        ).astype(jnp.bfloat16)
        pl.when(i == 0)(ring_z[0])
        return carry

    lax.fori_loop(0, side, keep, 0)
    ring_x[0]()
    ring_z[1]()
    ring_x[1]()

    def proj_in(step, total):
        chip_copy(step).wait_recv()
        return total + land_proj[step - 1]

    rows_sum[...] = lax.fori_loop(1, chips, proj_in, held_proj[chip]).reshape(rows_sum.shape)

    def sum_copy(step):
        return along_grp(
            step, rows_sum.at[(grp + step) % groups], land_grp.at[step - 1],
            grp_send.at[step], grp_recv.at[step],
        )

    for step in range(1, groups):
        sum_copy(step).start()
    mine = rows_sum[grp]
    for step in range(1, groups):
        sum_copy(step).wait_recv()
        mine = mine + land_grp[step - 1]
    proj_out[...] = mine

    mids[1] = (view_z(0, None)[...].astype(jnp.float32) + ring_z[2]()).astype(jnp.bfloat16)
    then_x[0]()
    mids[0] = (view_x(0, None)[...].astype(jnp.float32) + ring_x[2]()).astype(jnp.bfloat16)
    then_z[0]()
    then_x[1]()
    then_z[1]()
    whole = jnp.concatenate(
        [
            mids[0, z].astype(jnp.float32) + then_z[2](),
            mids[1, x].astype(jnp.float32) + then_x[2](),
        ],
        axis=1,
    )
    for n, ref in enumerate((gate_out, up_out, down_out)):
        ref[:, :main] = whole[:, n * main : (n + 1) * main]
        ref[:, main:] = whole[:, 3 * main + n * rest : 3 * main + (n + 1) * rest]

    def sent(step, carry):
        asks_copy(step, me).wait_send()
        pull_copy(step, me).wait_send()
        score_copy(step, me).wait_send()
        return carry

    lax.fori_loop(1, shards, sent, 0)
    for step in range(1, groups):
        sum_copy(step).wait_send()
    for j in range(4):
        rows_copy(j, False).wait_send()
        dout_copy(j, False).wait_send()
    for ring in (ring_x, ring_z, then_x, then_z):
        ring[3]()
    part_sent()
    query_swap(core).wait_send()

    def docs_out(c, carry):
        for j in range(4):
            docs_copies(c)(j, False).wait_send()
        return carry

    lax.fori_loop(0, chunks, docs_out, 0)
    proj_swap.wait_send()

    def swapped(i, carry):
        swap_copy(i).wait_send()
        return carry

    lax.fori_loop(0, side, swapped, 0)

    def chips_out(step, carry):
        chip_copy(step).wait_send()
        query_copy(step, chip).wait_send()
        return carry

    lax.fori_loop(1, chips, chips_out, 0)


def step_call(
    states, norm_gain, final_gain, w_gate, w_up, w_down_t, w_proj, cent_ids, lens, codes, bucket,
    tables, which, table, side, caps, q_len,
):
    groups = lax.axis_size("grp")
    shards = 2 * side * side
    chips = side * side
    tok_rows, width = states.shape
    part = w_gate.shape[0]
    dim = w_proj.shape[1]
    passages, toks = cent_ids.shape
    dims, count = table.shape
    chunks = 8
    block = width // shards
    tokens = groups * tok_rows
    vmem = pl.BlockSpec(memory_space=pltpu.VMEM)
    smem = pl.BlockSpec(memory_space=pltpu.SMEM)
    hbm = pl.BlockSpec(memory_space=pl.ANY)
    bf16, f32 = jnp.bfloat16, jnp.float32
    dma = pltpu.SemaphoreType.DMA
    wide = (side, side, block, -(-3 * part // 256) * 256)
    cols = wide[3] // 2
    return pl.pallas_call(
        functools.partial(step_kernel, side, groups, chunks),
        out_shape=(jax.ShapeDtypeStruct((8, 128), f32),)
        + (jax.ShapeDtypeStruct((block, part), f32),) * 3
        + (jax.ShapeDtypeStruct((block // groups, dim), f32),),
        in_specs=[vmem] * 3 + [hbm] * 3 + [vmem] + [smem] * 2 + [vmem] * 5 + [hbm],
        out_specs=(vmem,) * 5,
        scratch_shapes=[
            pltpu.VMEM((dims, count), bf16),
            pltpu.VMEM((4, dims, toks), f32),
            pltpu.VMEM((part, width), bf16),
            pltpu.VMEM((part, width), bf16),
            pltpu.VMEM((part, width), bf16),
            pltpu.VMEM((groups, passages, dims, toks), bf16),
            pltpu.VMEM((groups, tok_rows, width), bf16),
            pltpu.VMEM((groups, tok_rows, part), bf16),
            pltpu.VMEM((groups, tok_rows, part), bf16),
            pltpu.VMEM((groups, tok_rows, part), bf16),
            pltpu.VMEM((groups, tok_rows, width), bf16),
            pltpu.VMEM((tok_rows, width), f32),
            pltpu.VMEM((2, tok_rows // 2, width), bf16),
            pltpu.VMEM((2, tok_rows, width), bf16),
            pltpu.VMEM((tok_rows, width), f32),
            pltpu.VMEM((width, tok_rows), bf16),
            pltpu.VMEM((tok_rows, dim), f32),
            pltpu.VMEM((shards, 1, 128), jnp.int32),
            pltpu.SMEM((shards, 1, 128), jnp.int32),
            pltpu.VMEM((chips, 2, tok_rows // q_len, q_len, dim), bf16),
            pltpu.VMEM((shards, caps, q_len, dim), bf16),
            pltpu.VMEM((shards, 8, dim), f32),
            pltpu.VMEM((shards, caps, q_len, dim), bf16),
            pltpu.VMEM((shards, 8, dim), f32),
            pltpu.VMEM((tok_rows // q_len, shards, 8, dim), f32),
            pltpu.VMEM((groups, tok_rows, width), bf16),
            pltpu.VMEM((chips, 2, block, tokens), bf16),
            pltpu.VMEM((chips, 2, block, tokens), bf16),
            pltpu.VMEM((groups, tok_rows, part), bf16),
            pltpu.VMEM((groups, tok_rows, part), bf16),
            pltpu.VMEM(wide, bf16),
            pltpu.VMEM(wide, bf16),
            pltpu.VMEM(wide, bf16),
            pltpu.VMEM((2, 2, side // 2, block, cols), bf16),
            pltpu.VMEM((2, 2, side, block, cols), bf16),
            pltpu.VMEM((2, side, block, cols), bf16),
            pltpu.VMEM((2, 2, block // 2, cols), bf16),
            pltpu.VMEM((2, 2, block, cols), bf16),
            pltpu.VMEM((chips, 2, block, dim), f32),
            pltpu.VMEM((chips, block, dim), f32),
            pltpu.VMEM((chips, block, dim), f32),
            pltpu.VMEM((chips - 1, block, dim), f32),
            pltpu.VMEM((groups, block // groups, dim), f32),
            pltpu.VMEM((groups - 1, block // groups, dim), f32),
            dma((8,)),
            dma((3,)),
            dma,
        ]
        + [dma((groups,))] * 6
        + [dma((chunks, groups))] * 2
        + [dma((5, groups))] * 2
        + [dma((shards,))] * 6
        + [dma((side + 2,))] * 2
        + [dma((2, chips - 1))] * 2,
        compiler_params=pltpu.CompilerParams(
            collective_id=0, has_side_effects=True, vmem_limit_bytes=60 << 20
        ),
        cost_estimate=pl.CostEstimate(flops=0, bytes_accessed=300_000_000, transcendentals=0),
    )(
        states, norm_gain, final_gain, w_gate, w_up, w_down_t, w_proj, cent_ids >> 7, lens,
        cent_ids, codes, bucket, tables, which, table,
    )


def coords(shape):
    me = lax.axis_index("shard")
    return me // (2 * shape), (me // 2) % shape, me % 2, lax.axis_index("grp")


def ranks(hits):
    count = hits.shape[1]
    before = lax.broadcasted_iota(jnp.int32, (count, count), 0) < lax.broadcasted_iota(
        jnp.int32, (count, count), 1
    )
    return jnp.dot(
        hits.astype(jnp.bfloat16), before.astype(jnp.bfloat16), preferred_element_type=jnp.float32
    ).astype(jnp.int32)


def slots(hits, caps):
    nth = lax.broadcasted_iota(jnp.int32, (1, caps, 1), 1)
    return hits[:, None, :] & (ranks(hits)[:, None, :] == nth)


def local(
    query_states,
    norm_gain,
    final_gain,
    w_gate,
    w_up,
    w_down_t,
    w_proj,
    centroids,
    bucket_values,
    centroid_ids,
    residual_codes,
    passage_lens,
    negative_ids,
):
    q_dev, q_len, width = query_states.shape
    dim = w_proj.shape[1]
    shards = lax.axis_size("shard")
    side = math.isqrt(shards // 2)
    cands = negative_ids.shape[1]
    tok_rows = q_dev * q_len
    local_pass = centroid_ids.shape[0]
    caps = 2 * q_dev * cands // shards
    me = lax.axis_index("shard")

    flat_ids = negative_ids.reshape(1, -1)
    owner = lax.broadcasted_iota(jnp.int32, (shards, 1), 0)
    places = lax.broadcasted_iota(jnp.int32, (1, 1, q_dev * cands), 2)
    sent = slots(flat_ids // local_pass == owner, caps)
    place = jnp.sum(jnp.where(sent, places, 0), axis=2)
    asked = jnp.sum(jnp.where(sent, (flat_ids % local_pass)[:, None, :], 0), axis=2)
    tables = jnp.concatenate(
        [asked, place // cands, jnp.zeros((shards, 128 - 2 * caps), jnp.int32)], axis=1
    ).reshape(shards, 1, 128)
    lens = lax.dynamic_slice(passage_lens, (me * local_pass,), (local_pass,))
    states = query_states.reshape(tok_rows, width)
    filled = jnp.any(sent, axis=2)[:, :, None]
    query = lax.broadcasted_iota(jnp.int32, (1, 1, 128), 2)
    mine = filled & ((place // cands)[:, :, None] == query)
    first = mine & ((place % cands)[:, :, None] == 0)
    which = mine.astype(jnp.int32) + first.astype(jnp.int32)
    which = jnp.pad(which, ((0, 0), (0, 8 - caps), (0, 0))).reshape(shards * 8, 128)
    losses, grad_gate, grad_up, grad_down, grad_proj = step_call(
        states, norm_gain.reshape(1, -1), final_gain.reshape(1, -1), w_gate.T, w_up.T, w_down_t.T,
        w_proj, centroid_ids, lens, residual_codes, bucket_values, tables, which, centroids, side,
        caps, q_len,
    )
    return (losses[0, :q_dev], grad_gate, grad_up, grad_down, grad_proj)


def solution(mesh):
    placed = (
        P(("shard", "grp"), None, None),
        P(),
        P(),
        P(None, "grp"),
        P(None, "grp"),
        P(None, "grp"),
        P(),
        P("grp", None),
        P(None, "grp"),
        P("shard", None),
        P("shard", "grp", None),
        P(),
        P(("shard", "grp"), None),
    )
    return jax.shard_map(
        local,
        mesh=mesh,
        in_specs=placed,
        out_specs=(
            P(("shard", "grp")),
            P("shard", "grp"),
            P("shard", "grp"),
            P("shard", "grp"),
            P(("shard", "grp"), None),
        ),
        check_vma=False,
    )
```
